128 devices in a mesh: front: 4 (over z), row: 4 (over x), col: 8 (over y, core).
Axes of the slice: x: 4, y: 4, z: 4, core: 2. Of those that a mesh axis runs over, the one named last changes fastest.
Arguments:
- child_fronts: float32 [4, 6, 4, 3, 8, 128, 128], P('front', None, 'row', None, 'col'), as said below
- parent_front: float32 [2, 16, 4, 8, 128, 128], P(None, ('front', 'row'), None, 'col'), as said below
- child_maps: int32 [4, 16], replicated, may hold values from 0 to 31, as said below
Outputs:
- child_factors: float32 [4, 6, 4, 3, 8, 128, 128], P('front', None, 'row', None, 'col')
- parent_factor: float32 [2, 16, 4, 8, 128, 128], P(None, ('front', 'row'), None, 'col')
The draws below stay inside these ranges and needn't reach their ends.
Inputs may be any that keep to these rules, and one draw needn't show every extreme that they name: `child_maps`: row f lists the parent blocks that receive child f's update blocks, strictly increasing; it starts at 0 and ends at 31. `child_fronts`: each front is symmetric positive definite. `parent_front`: symmetric positive definite.
All inputs are finite; a program needn't handle non-finite values.
Results may differ from the reference program's by a relative error of at most 0.0001.
Values sent between devices are 32-bit elements; how exact they have to be, the bound alone decides.
No kernel may reach another device: no remote copies, remote signals or barrier semaphores. Data moves between devices by JAX's collectives and lax.ppermute only.
A program may use at most 64 MiB of HBM per device.

```python
import jax
import jax.numpy as jnp
from jax import lax

BS = 128
NCB = 24
KCB = 8
NPB = 32
KPB = 6
FRONTS = 4
NUB = 16
CR = 6
CC = 3
PG = 16
PR = 2
PC = 4


def symmetric(key, order):
    first = jax.random.fold_in(key, 0)
    raw = jax.random.normal(first, (order, order), jnp.float32)
    mixed = raw + 0.9 * jnp.roll(raw, -1, axis=0)
    gram = jnp.dot(mixed, mixed.T, precision=lax.Precision.HIGHEST) / order
    gram = 0.5 * (gram + gram.T)
    matrix = gram + 0.2 * jnp.eye(order, dtype=jnp.float32)
    return matrix


def draw_child_fronts(key, part):
    keys = jax.random.split(key, FRONTS)
    order = NCB * BS
    matrices = jnp.stack([symmetric(keys[index_at], order) for index_at in range(FRONTS)])
    shaped = matrices.reshape(FRONTS, CR, NCB // CR, BS, CC, NCB // CC, BS)
    return jnp.transpose(shaped, (0, 1, 2, 4, 5, 3, 6))


def draw_parent_front(key, part):
    matrix = symmetric(jax.random.fold_in(key, 7), NPB * BS)
    shaped = matrix.reshape(PR, PG, BS, PC, NPB // PC, BS)
    return jnp.transpose(shaped, (0, 1, 3, 4, 2, 5))


def draw_child_maps(key, part):
    rows_out = []
    for index_at in range(FRONTS):
        shuffled = jax.random.permutation(jax.random.fold_in(key, index_at + 11), NPB - 2)
        chosen = jnp.concatenate([jnp.ones((1,), bool), shuffled < NUB - 2, jnp.ones((1,), bool)])
        rows_out.append(jnp.nonzero(chosen, size=NUB)[0].astype(jnp.int32))
    return jnp.stack(rows_out)


def setup_inputs(seed: int = 0) -> dict:
    splits = jax.random.split(jax.random.key(seed), 4)
    return {
        "child_fronts": draw_child_fronts(jax.random.fold_in(splits[3], 71), 0),
        "parent_front": draw_parent_front(jax.random.fold_in(splits[3], 71), 0),
        "child_maps": draw_child_maps(jax.random.fold_in(splits[3], 71), 0),
    }


precise = lax.Precision.HIGHEST

def panel_solve(blocks, step_at):
    block_count = blocks.shape[0]
    block_size = blocks.shape[1]
    diag_block = lax.dynamic_index_in_dim(blocks, step_at, 0, keepdims=False)
    lower_part = jnp.linalg.cholesky(diag_block)
    stacked = jnp.transpose(blocks, (2, 0, 1)).reshape(block_size, block_count * block_size)
    solved = lax.linalg.triangular_solve(lower_part, stacked, left_side=True, lower=True)
    solved = solved.reshape(block_size, block_count, block_size)
    place_idx = jnp.arange(block_count)[None, :, None]
    factor = jnp.where(place_idx == step_at, jnp.transpose(lower_part)[:, None, :], solved)
    return jnp.where(place_idx < step_at, jnp.zeros_like(factor), factor)

def eliminate(matrix, pivots):
    block_count = matrix.shape[0] // BS
    row_block = jnp.arange(block_count * BS) // BS
    for step_at in range(pivots):
        blocks = matrix[:, step_at * BS:(step_at + 1) * BS].reshape(block_count, BS, BS)
        factor = panel_solve(blocks, step_at)
        tall = jnp.transpose(factor, (1, 2, 0)).reshape(block_count * BS, BS)
        below_part = jnp.where(row_block[:, None] > step_at, tall, jnp.zeros_like(tall))
        matrix = matrix - jnp.dot(below_part, below_part.T, precision=precise)
        matrix = matrix.at[:, step_at * BS:(step_at + 1) * BS].set(tall)
    keep_mask = (row_block[:, None] >= row_block[None, :]) | (row_block[:, None] >= pivots)
    return jnp.where(keep_mask, matrix, jnp.zeros_like(matrix))

def to_full(layout):
    lead_rows, grid_rows, lead_cols, grid_cols = (layout.shape[0], layout.shape[1], layout.shape[2], layout.shape[3])
    return jnp.transpose(layout, (0, 1, 4, 2, 3, 5)).reshape(lead_rows * grid_rows * BS, lead_cols * grid_cols * BS)

def to_layout(matrix, lead_rows, grid_rows, lead_cols, grid_cols):
    shaped = matrix.reshape(lead_rows, grid_rows, BS, lead_cols, grid_cols, BS)
    return jnp.transpose(shaped, (0, 1, 3, 4, 2, 5))

def reference(child_fronts, parent_front, child_maps):
    finished = []
    assembled = to_full(parent_front)
    offsets = jnp.arange(BS, dtype=jnp.int32)
    for front_idx in range(FRONTS):
        layout = child_fronts[front_idx]
        factored = eliminate(to_full(layout), KCB)
        finished.append(to_layout(factored, layout.shape[0], layout.shape[1], layout.shape[2], layout.shape[3]))
        trailing = factored[KCB * BS:, KCB * BS:]
        targets = (child_maps[front_idx][:, None] * BS + offsets[None, :]).reshape(-1).astype(jnp.int32)
        assembled = assembled.at[targets[:, None], targets[None, :]].add(trailing)
    parent_done = eliminate(assembled, KPB)
    shape_of = parent_front.shape
    return (jnp.stack(finished), to_layout(parent_done, shape_of[0], shape_of[1], shape_of[2], shape_of[3]))
```

```python
import functools

import jax
import jax.numpy as jnp
from jax import lax
from jax.experimental import pallas as pl
from jax.experimental.pallas import tpu as pltpu
from jax.sharding import PartitionSpec as P

BS = 128
KCB = 8
KPB = 6
F32 = jnp.float32
BF16 = jnp.bfloat16
ALL = ("front", "row", "col")
LOWER = [(i, j) for i in range(KPB) for j in range(i + 1)]
VMEM_BYTES = 56 * 1024 * 1024


def split(x):
    high = x.astype(BF16)
    low = (x - high.astype(F32)).astype(BF16)
    return high, low


def dot3(a, b, dims):
    def one(x, y):
        return lax.dot_general(x, y, (dims, ((), ())), preferred_element_type=F32)

    return one(a[0], b[0]) + (one(a[0], b[1]) + one(a[1], b[0]))


NT = ((1,), (1,))
NN = ((1,), (0,))


def factor_block(load, store_upper, store_inverse):
    panels = BS // 8
    full = (8, BS)
    sub = lax.broadcasted_iota(jnp.int32, full, 0)
    lane = lax.broadcasted_iota(jnp.int32, full, 1)
    rest = [load(t) for t in range(panels)]
    inverse = [jnp.where(lane == sub + 8 * t, 1.0, 0.0).astype(F32) for t in range(panels)]
    for p in range(panels):
        at = 8 * p
        pivot_rows = rest[p]
        columns = [jnp.broadcast_to(pivot_rows[:, at + i : at + i + 1], full) for i in range(8)]
        e = {}
        for i in range(8):
            for k in range(i, 8):
                e[k, i] = jnp.broadcast_to(columns[i][k : k + 1, :], full)
        c = {}
        for t in range(p + 1, panels):
            for i in range(8):
                c[t, i] = jnp.broadcast_to(rest[t][:, at + i : at + i + 1], full)
        n = {}
        for i in range(8):
            scale = lax.rsqrt(e[i, i])
            n[i, i] = scale
            for k in range(i + 1, 8):
                e[k, i] = e[k, i] * scale
            for k in range(i + 1, 8):
                for j in range(i + 1, k + 1):
                    e[k, j] = e[k, j] - e[k, i] * e[j, i]
            for k in range(i):
                total = e[i, k] * n[k, k]
                for m in range(k + 1, i):
                    total = total + e[i, m] * n[m, k]
                n[i, k] = -(total * scale)

        def forward(x):
            source = [jnp.broadcast_to(x[k : k + 1, :], full) for k in range(8)]
            solved = []
            for i in range(8):
                total = n[i, 0] * source[0]
                for k in range(1, i + 1):
                    total = total + n[i, k] * source[k]
                solved.append(total)
            joined = solved[0]
            for i in range(1, 8):
                joined = jnp.where(sub == i, solved[i], joined)
            return solved, joined

        def backward(solved):
            out = []
            for i in range(8):
                total = n[i, i] * solved[i]
                for k in range(i + 1, 8):
                    total = total + n[k, i] * solved[k]
                out.append(total)
            return out

        upper_rows, upper = forward(pivot_rows)
        inverse_rows, inverse_out = forward(inverse[p])
        store_upper(p, jnp.where(lane >= sub + at, upper, 0.0))
        store_inverse(p, inverse_out)
        if p + 1 < panels:
            upper_rows = backward(upper_rows)
            inverse_rows = backward(inverse_rows)
            for t in range(p + 1, panels):
                first = c[t, 0] * upper_rows[0]
                second = c[t, 0] * inverse_rows[0]
                for i in range(1, 8):
                    first = first + c[t, i] * upper_rows[i]
                    second = second + c[t, i] * inverse_rows[i]
                rest[t] = rest[t] - first
                inverse[t] = inverse[t] - second


def factor_pivots(pivots, work, upper, lower_high, lower_low, inverse, inverse_high, inverse_low):
    for k in range(pivots):
        here = slice(k * BS, (k + 1) * BS)

        def load(t):
            return work[k * BS + 8 * t : k * BS + 8 * t + 8, here]

        def store_upper(t, x):
            upper[8 * t : 8 * t + 8, :] = x

        def store_inverse(t, x):
            inverse[8 * t : 8 * t + 8, :] = x

        factor_block(load, store_upper, store_inverse)
        work[here, here] = jnp.transpose(upper[...])
        inv = split(inverse[...])
        inverse_high[k] = inv[0]
        inverse_low[k] = inv[1]
        if k + 1 < pivots:
            below = slice((k + 1) * BS, pivots * BS)
            panel = dot3(split(work[below, here]), inv, NT)
            work[below, here] = panel
            high, low = split(panel)
            lower_high[below, here] = high
            lower_low[below, here] = low
            for j in range(k + 1, pivots, 1 if k + 1 == pivots - 1 else 2):
                wide = min(2, pivots - j)
                rows = slice(j * BS, pivots * BS)
                cols = slice(j * BS, (j + wide) * BS)
                left = (lower_high[rows, here], lower_low[rows, here])
                right = (lower_high[cols, here], lower_low[cols, here])
                work[rows, cols] = work[rows, cols] - dot3(left, right, NT)


def child_pivots_kernel(where, blocks, lower_high, lower_low, inverse_high, inverse_low, own, work, upper, inverse):
    row, col = where[0], where[1]
    for i in range(KCB):
        for j in range(i + 1):
            work[i * BS : (i + 1) * BS, j * BS : (j + 1) * BS] = blocks[i % 4, j, i // 4]
    factor_pivots(KCB, work, upper, lower_high, lower_low, inverse, inverse_high, inverse_low)
    for i in range(2):
        at = row + 4 * i
        block = work[pl.ds(pl.multiple_of(at * BS, BS), BS), pl.ds(pl.multiple_of(col * BS, BS), BS)]
        own[i] = jnp.where(at >= col, block, 0.0)


def child_panels_kernel(
    where, lower_high, lower_low, inverse_high, inverse_low, rows_in, cols_in, trailing, own, parent,
    out, slices, rows_work, cols_work, rows_done, rows_high, rows_low, cols_high, cols_low
):
    col = where[1]
    for k in range(KCB):
        here = slice(k * BS, (k + 1) * BS)
        rows_work[:, here] = rows_in[k]
        for j in range(2):
            cols_work[here, j * BS : (j + 1) * BS] = cols_in[k % 4, k // 4, j]
    for k in range(KCB):
        here = slice(k * BS, (k + 1) * BS)
        inv = (inverse_high[k], inverse_low[k])
        solved = dot3(split(rows_work[:, here]), inv, NT)
        rows_done[k] = solved
        rows = split(solved)
        rows_high[:, here] = rows[0]
        rows_low[:, here] = rows[1]
        cols = split(dot3(inv, split(cols_work[here, :]), NN))
        cols_high[here, :] = cols[0]
        cols_low[here, :] = cols[1]
        if k + 1 < KCB:
            below = slice((k + 1) * BS, KCB * BS)
            lower = (lower_high[below, here], lower_low[below, here])
            rows_work[:, below] = rows_work[:, below] - dot3(rows, lower, NT)
            cols_work[below, :] = cols_work[below, :] - dot3(lower, cols, NN)
    delta = dot3((rows_high[...], rows_low[...]), (cols_high[...], cols_low[...]), NN)
    zero = jnp.zeros((BS, BS), F32)
    for i in range(2):
        out[i, 0] = own[i]
        for j in range(2):
            out[i, 1 + j] = zero
    for i in range(4):
        out[2 + i, 0] = rows_done[col, i * BS : (i + 1) * BS, :]
        for j in range(2):
            block = trailing[i, j] - delta[i * BS : (i + 1) * BS, j * BS : (j + 1) * BS]
            out[2 + i, 1 + j] = block
            slices[pl.ds(2 * i + j, BS, stride=16), :] = block
    for i in range(2):
        for j in range(4):
            slices[pl.ds(8 + 4 * i + j, BS, stride=16), :] = parent[i, j]


def extend_add_kernel(maps, came, out, pivot_rows, panel_rows):
    out[:, 0:8, :] = came[:, 8:16, :]

    def one_row(step, carry):
        front, u = step // 16, step % 16
        target_row = maps[front, u]
        row_at = (target_row % 16) * 8
        place_at = (target_row // 16) * 4
        source_at = (front * 4 + u % 4) * 8
        source_place = (u // 4) * 2
        targets = []
        totals = []
        for v in range(16):
            target_col = maps[front, v]
            at = row_at + target_col % 8
            place = place_at + target_col // 8
            targets.append((at, place))
            totals.append(
                out[at, pl.ds(place, 1), :] + came[source_at + v % 8, pl.ds(source_place + v // 8, 1), :]
            )
        for (at, place), total in zip(targets, totals):
            out[at, pl.ds(place, 1), :] = total
        return carry

    lax.fori_loop(0, 64, one_row, 0)
    pivot_rows[...] = jnp.zeros_like(pivot_rows)
    panel_rows[...] = jnp.zeros_like(panel_rows)
    for q, (i, j) in enumerate(LOWER):
        pivot_rows[q : q + 1, :] = out[i * 8 + j, 0:1, :]
    out[:, 16:40, :] = jnp.broadcast_to(pivot_rows[...][None], (128, 24, BS))
    for j in range(32):
        for k in range(KPB):
            panel_rows[k : k + 1, :] = out[(j % 16) * 8 + k, (j // 16) * 4 : (j // 16) * 4 + 1, :]
        for f in range(4):
            out[(f * 4 + j // 8) * 8 + j % 8, 8:16, :] = panel_rows[...]


def collect_kernel(came, own, panel):
    for b in range(8):
        own[b] = came[pl.ds(b, BS, stride=40), :]
    for b in range(KPB):
        panel[b] = came[pl.ds(8 + b, BS, stride=40), :]


def parent_pivots_kernel(where, came, lower_high, lower_low, inverse_high, inverse_low, own, work, upper, inverse):
    group, col = where[0], where[1]
    for q, (i, j) in enumerate(LOWER):
        work[i * BS : (i + 1) * BS, j * BS : (j + 1) * BS] = came[pl.ds(16 + q, BS, stride=40), :]
    factor_pivots(KPB, work, upper, lower_high, lower_low, inverse, inverse_high, inverse_low)
    row = jnp.minimum(group, KPB - 1)
    at = jnp.minimum(col, KPB - 1)
    block = work[pl.ds(pl.multiple_of(row * BS, BS), BS), pl.ds(pl.multiple_of(at * BS, BS), BS)]
    own[...] = jnp.where(row >= at, block, 0.0)


def parent_panels_kernel(
    where, lower_high, lower_low, inverse_high, inverse_low, rows_in, cols_in, blocks, own,
    out, work, done, done_high, done_low
):
    group, col = where[0], where[1]
    for k in range(KPB):
        here = slice(k * BS, (k + 1) * BS)
        for i in range(2):
            work[i * BS : (i + 1) * BS, here] = rows_in[k, i]
        for j in range(4):
            work[(2 + j) * BS : (3 + j) * BS, here] = cols_in[j, k]
    for k in range(KPB):
        here = slice(k * BS, (k + 1) * BS)
        solved = dot3(split(work[:, here]), (inverse_high[k], inverse_low[k]), NT)
        done[k] = solved[0 : 2 * BS, :]
        rows = split(solved)
        done_high[:, here] = rows[0]
        done_low[:, here] = rows[1]
        if k + 1 < KPB:
            below = slice((k + 1) * BS, KPB * BS)
            lower = (lower_high[below, here], lower_low[below, here])
            work[:, below] = work[:, below] - dot3(rows, lower, NT)
    left = (done_high[0 : 2 * BS, :], done_low[0 : 2 * BS, :])
    right = (done_high[2 * BS :, :], done_low[2 * BS :, :])
    delta = dot3(left, right, NT)
    at = jnp.minimum(col, KPB - 1)
    for i in range(2):
        row_pivot = group + 16 * i < KPB
        for j in range(4):
            col_pivot = col + 8 * j < KPB
            updated = blocks[i, j] - delta[i * BS : (i + 1) * BS, j * BS : (j + 1) * BS]
            if i == 0:
                updated = jnp.where(row_pivot, 0.0, updated)
            if j == 0:
                column = done[at, i * BS : (i + 1) * BS, :]
                if i == 0:
                    column = jnp.where(row_pivot, own[...], column)
                updated = jnp.where(col_pivot, column, updated)
            out[i, j] = updated


def call(kernel, outs, scratch, name, flops=0):
    def run(*args, smem=1):
        specs = [pl.BlockSpec(memory_space=pltpu.SMEM)] * smem
        specs += [pl.BlockSpec(memory_space=pltpu.VMEM)] * (len(args) - smem)
        size = sum(a.size * a.dtype.itemsize for a in args)
        return pl.pallas_call(
            kernel,
            out_shape=[jax.ShapeDtypeStruct(s, t) for s, t in outs],
            in_specs=specs,
            out_specs=[pl.BlockSpec(memory_space=pltpu.VMEM)] * len(outs),
            scratch_shapes=[pltpu.VMEM(s, t) for s, t in scratch],
            compiler_params=pltpu.CompilerParams(vmem_limit_bytes=VMEM_BYTES),
            cost_estimate=pl.CostEstimate(flops=flops, bytes_accessed=size, transcendentals=0),
            name=name,
        )(*args)

    return run


def pivots_call(kernel, pivots, own_shape, name):
    n = pivots * BS
    return call(
        kernel,
        [((n, n), BF16), ((n, n), BF16), ((pivots, BS, BS), BF16), ((pivots, BS, BS), BF16), (own_shape, F32)],
        [((n, n), F32), ((BS, BS), F32), ((BS, BS), F32)],
        name,
        flops=30_000_000_000,
    )


def shards(child_fronts, parent_front, child_maps):
    front = lax.axis_index("front")
    row = lax.axis_index("row")
    col = lax.axis_index("col")
    child = child_fronts.reshape(6, 3, BS, BS)
    parent = parent_front.reshape(2, 4, BS, BS)
    where = jnp.stack([row, col]).astype(jnp.int32)
    group_where = jnp.stack([front * 4 + row, col]).astype(jnp.int32)

    pivots = lax.all_gather(child[0:2, 0], ("row", "col"), axis=0)
    pivots, rows_in, cols_in = lax.optimization_barrier((pivots, child[2:, 0], child[0:2, 1:]))
    rows_in = lax.all_gather(rows_in, "col", axis=0)
    cols_in = lax.all_gather(cols_in, "row", axis=0)

    factors = pivots_call(child_pivots_kernel, KCB, (2, BS, BS), "child_pivots")(
        where, pivots.reshape(4, 8, 2, BS, BS)
    )
    n = KCB * BS
    child_done, slices = call(
        child_panels_kernel,
        [((6, 3, BS, BS), F32), ((BS * 16, BS), F32)],
        [
            ((512, n), F32), ((n, 256), F32), ((KCB, 512, BS), F32),
            ((512, n), BF16), ((512, n), BF16), ((n, 256), BF16), ((n, 256), BF16),
        ],
        "child_panels",
        flops=3_000_000_000,
    )(where, *factors[:4], rows_in.reshape(KCB, 512, BS), cols_in, child[2:, 1:], factors[4], parent)

    came = lax.all_to_all(slices.reshape(128, 16, BS), ALL, 0, 0, tiled=True)
    (sent,) = call(
        extend_add_kernel,
        [((128, 40, BS), F32)],
        [((24, BS), F32), ((8, BS), F32)],
        "extend_add",
    )(child_maps, came)
    came = lax.all_to_all(sent, ALL, 0, 0, tiled=True).reshape(128 * 40, BS)
    blocks, panel = call(collect_kernel, [((8, BS, BS), F32), ((KPB, BS, BS), F32)], [], "collect")(came, smem=0)
    blocks = blocks.reshape(2, 4, BS, BS)
    rows_in = lax.all_gather(blocks[:, 0], "col", axis=0)
    cols_in = lax.all_gather(panel, "row", axis=0)
    factors = pivots_call(parent_pivots_kernel, KPB, (BS, BS), "parent_pivots")(group_where, came)
    n = KPB * BS
    (parent_done,) = call(
        parent_panels_kernel,
        [((2, 4, BS, BS), F32)],
        [((n, n), F32), ((KPB, 256, BS), F32), ((n, n), BF16), ((n, n), BF16)],
        "parent_panels",
        flops=3_000_000_000,
    )(group_where, *factors[:4], rows_in, cols_in, blocks, factors[4])
    return child_done.reshape(child_fronts.shape), parent_done.reshape(parent_front.shape)


def solution(mesh):
    in_specs = (
        P("front", None, "row", None, "col", None, None),
        P(None, ("front", "row"), None, "col", None, None),
        P(),
    )
    out_specs = (
        P("front", None, "row", None, "col", None, None),
        P(None, ("front", "row"), None, "col", None, None),
    )
    return jax.shard_map(shards, mesh=mesh, in_specs=in_specs, out_specs=out_specs, check_vma=False)
```

```python
import functools

import jax
import jax.numpy as jnp
from jax import lax
from jax.experimental import pallas as pl
from jax.experimental.pallas import tpu as pltpu
from jax.sharding import PartitionSpec as P

BS = 128
KCB = 8
KPB = 6
F32 = jnp.float32
BF16 = jnp.bfloat16
COL = ("y", "core")
ALL = ("front", "row", "y", "core")
SLOTS = 40
LOWER = [(i, j) for i in range(KPB) for j in range(i + 1)]
MIB = 1024 * 1024


def split(x):
    high = x.astype(BF16)
    low = (x - high.astype(F32)).astype(BF16)
    return high, low


def dot3(a, b, dims):
    def one(x, y):
        return lax.dot_general(x, y, (dims, ((), ())), preferred_element_type=F32)

    return one(a[0], b[0]) + (one(a[0], b[1]) + one(a[1], b[0]))


NT = ((1,), (1,))
NN = ((1,), (0,))


def tree_sum(terms):
    terms = list(terms)
    while len(terms) > 1:
        terms = [sum(terms[i + 1 : i + 2], terms[i]) for i in range(0, len(terms), 2)]
    return terms[0]


def factor_block(load, store_upper, store_inverse, elements, between=lambda p: None):
    panels = BS // 8
    full = (8, BS)
    sub = lax.broadcasted_iota(jnp.int32, full, 0)
    lane = lax.broadcasted_iota(jnp.int32, full, 1)
    rest = [load(t) for t in range(panels)]
    inverse = [jnp.where(lane == sub + 8 * t, 1.0, 0.0).astype(F32) for t in range(panels)]
    for p in range(panels):
        at = 8 * p
        pivot_rows = rest[p]
        for i in range(8):
            elements[p % 2, i] = jnp.broadcast_to(pivot_rows[:, at + i : at + i + 1], full)
        e = {}
        for i in range(8):
            for k in range(i, 8):
                e[k, i] = jnp.broadcast_to(elements[p % 2, i, k : k + 1, :], full)
        c = {}
        for t in range(p + 1, panels):
            for i in range(8):
                c[t, i] = jnp.broadcast_to(rest[t][:, at + i : at + i + 1], full)
        unit, n, root, over = {}, {}, {}, {}
        for i in range(8):
            over[i] = pl.reciprocal(e[i, i])
            root[i] = lax.rsqrt(e[i, i])
            for k in range(i + 1, 8):
                unit[k, i] = e[k, i] * over[i]
                for j in range(i + 1, k + 1):
                    e[k, j] = e[k, j] - unit[k, i] * e[j, i]
            for k in range(i):
                total = unit[i, k]
                for m in range(k + 1, i):
                    total = total + unit[i, m] * n[m, k]
                n[i, k] = -total

        def forward(x):
            source = [jnp.broadcast_to(x[k : k + 1, :], full) for k in range(8)]
            solved = [tree_sum([n[i, k] * source[k] for k in range(i)] + [source[i]]) for i in range(8)]
            joined = solved[0] * root[0]
            for i in range(1, 8):
                joined = jnp.where(sub == i, solved[i] * root[i], joined)
            return solved, joined

        def backward(solved):
            scaled = [solved[i] * over[i] for i in range(8)]
            return [tree_sum([scaled[i]] + [n[k, i] * scaled[k] for k in range(i + 1, 8)]) for i in range(8)]

        upper_rows, upper = forward(pivot_rows)
        inverse_rows, inverse_out = forward(inverse[p])
        store_upper(p, jnp.where(lane >= sub + at, upper, 0.0))
        store_inverse(p, inverse_out)
        if p + 1 < panels:
            upper_rows = backward(upper_rows)
            inverse_rows = backward(inverse_rows)
            for t in range(p + 1, panels):
                rest[t] = rest[t] - tree_sum([c[t, i] * upper_rows[i] for i in range(8)])
                inverse[t] = inverse[t] - tree_sum([c[t, i] * inverse_rows[i] for i in range(8)])
        between(p)


def factor_pivots(
    pivots, work, upper, lower_high, lower_low, inverse, inverse_high, inverse_low, elements
):
    def blk(i, count=1):
        return slice(i * BS, (i + count) * BS)

    def panel(rows, here, inv):
        solved = dot3(split(work[rows, here]), inv, NT)
        work[rows, here] = solved
        high, low = split(solved)
        lower_high[rows, here] = high
        lower_low[rows, here] = low

    def update(rows, cols, here):
        left = (lower_high[rows, here], lower_low[rows, here])
        right = (lower_high[cols, here], lower_low[cols, here])
        work[rows, cols] = work[rows, cols] - dot3(left, right, NT)

    waiting = []
    for k in range(pivots):
        here = blk(k)

        def load(t):
            return work[k * BS + 8 * t : k * BS + 8 * t + 8, here]

        def store_upper(t, x):
            upper[8 * t : 8 * t + 8, :] = x

        def store_inverse(t, x):
            inverse[8 * t : 8 * t + 8, :] = x

        share = -(-len(waiting) // 12)

        def between(p):
            for _ in range(share):
                if waiting:
                    waiting.pop(0)()

        factor_block(load, store_upper, store_inverse, elements, between)
        inv = split(inverse[...])
        inverse_high[k] = inv[0]
        inverse_low[k] = inv[1]
        if k + 1 < pivots:
            panel(blk(k + 1), here, inv)
            update(blk(k + 1), blk(k + 1), here)
        work[here, here] = jnp.transpose(upper[...])
        if k + 2 < pivots:
            after = slice((k + 2) * BS, pivots * BS)
            waiting.append(functools.partial(panel, after, here, inv))
            waiting.append(functools.partial(update, after, blk(k + 1), here))
            for j in range(k + 2, pivots, 2):
                wide = min(2, pivots - j)
                for i in range(j, pivots, 2):
                    tall = min(2, pivots - i)
                    waiting.append(functools.partial(update, blk(i, tall), blk(j, wide), here))


def own_col():
    return lax.axis_index("y") * 2 + lax.axis_index("core")


def prepare_kernel(child, payload, rows_out, cols_out):
    row, col = lax.axis_index("row"), own_col()
    half = BS // 2
    here = lax.broadcasted_iota(jnp.int32, (half, BS), 0)
    lane = lax.broadcasted_iota(jnp.int32, (half, BS), 1)
    for s in range(2):
        block = child[s, 0]
        at = row + 4 * s
        top, bottom = block[:half], block[half:]
        turned = jnp.transpose(block)[half:]
        packed = jnp.where((lane < half) | (lane - half > here), bottom, pltpu.roll(top, half, 1))
        sent = jnp.where(at > col, top, jnp.where(at < col, turned, packed))
        payload[0, s * half : (s + 1) * half, :] = sent
        diagonal = jnp.sum(jnp.where(lane - half == here, bottom, 0.0), axis=0, keepdims=True)

        @pl.when(at == col)
        def _():
            payload[0, BS : BS + 8, :] = jnp.broadcast_to(diagonal, (8, BS))

    @pl.when((row != col) & (row + 4 != col))
    def _():
        payload[0, BS : BS + 8, :] = jnp.zeros((8, BS), F32)

    for d in range(1, 16):
        payload[d] = payload[0]
    for i in range(4):
        rows_out[i] = child[2 + i, 0]
    for i in range(2):
        for j in range(2):
            cols_out[i, j] = child[i, 1 + j]


def child_pivots_kernel(
    mine, other, lower_high, lower_low, inverse_high, inverse_low, own, work, upper, inverse, elements
):
    row, col, core = lax.axis_index("row"), own_col(), lax.axis_index("core")
    half = BS // 2
    here = lax.broadcasted_iota(jnp.int32, (half, BS), 0)
    lane = lax.broadcasted_iota(jnp.int32, (half, BS), 1)
    eye = lax.broadcasted_iota(jnp.int32, (BS, BS), 0) == lax.broadcasted_iota(jnp.int32, (BS, BS), 1)

    def received(i, j, rows):
        at = (i % 4) * 4 + j // 2
        return jnp.where(core == j % 2, mine[at, rows, :], other[at, rows, :])

    def piece(i, j):
        return received(i, j, slice((i // 4) * half, (i // 4 + 1) * half))

    for i in range(KCB):
        packed = piece(i, i)
        diagonal = received(i, i, slice(BS, BS + 1))
        at = slice(i * BS, (i + 1) * BS)
        work[i * BS : i * BS + half, at] = jnp.where(lane <= here, pltpu.roll(packed, half, 1), 0.0)
        work[i * BS + half : (i + 1) * BS, at] = jnp.where(
            (lane < half) | (lane - half > here), packed, jnp.where(lane - half == here, diagonal, 0.0)
        )
        part = work[at, at]
        work[at, at] = part + jnp.where(eye, 0.0, jnp.transpose(part))
        for j in range(i):
            work[i * BS : i * BS + half, j * BS : (j + 1) * BS] = piece(i, j)
            work[i * BS + half : (i + 1) * BS, j * BS : (j + 1) * BS] = piece(j, i)
    factor_pivots(
        KCB, work, upper, lower_high, lower_low, inverse, inverse_high, inverse_low, elements
    )
    for i in range(2):
        at = row + 4 * i
        block = work[pl.ds(pl.multiple_of(at * BS, BS), BS), pl.ds(pl.multiple_of(col * BS, BS), BS)]
        own[i] = jnp.where(at >= col, block, 0.0)


def child_panels_kernel(
    lower_high, lower_low, inverse_high, inverse_low, rows_in, cols_in, child, own, parent,
    out, slices, rows_work, cols_work, rows_done, rows_high, rows_low, cols_high, cols_low
):
    col = own_col()
    for k in range(KCB):
        here = slice(k * BS, (k + 1) * BS)
        rows_work[:, here] = rows_in[k]
        for j in range(2):
            cols_work[here, j * BS : (j + 1) * BS] = cols_in[k % 4, k // 4, j]
    for k in range(KCB):
        here = slice(k * BS, (k + 1) * BS)
        inv = (inverse_high[k], inverse_low[k])
        solved = dot3(split(rows_work[:, here]), inv, NT)
        rows_done[k] = solved
        rows = split(solved)
        rows_high[:, here] = rows[0]
        rows_low[:, here] = rows[1]
        cols = split(dot3(inv, split(cols_work[here, :]), NN))
        cols_high[here, :] = cols[0]
        cols_low[here, :] = cols[1]
        if k + 1 < KCB:
            below = slice((k + 1) * BS, KCB * BS)
            lower = (lower_high[below, here], lower_low[below, here])
            rows_work[:, below] = rows_work[:, below] - dot3(rows, lower, NT)
            cols_work[below, :] = cols_work[below, :] - dot3(lower, cols, NN)
    delta = dot3((rows_high[...], rows_low[...]), (cols_high[...], cols_low[...]), NN)
    zero = jnp.zeros((BS, BS), F32)
    for i in range(2):
        out[i, 0] = own[i]
        for j in range(2):
            out[i, 1 + j] = zero
    for i in range(4):
        out[2 + i, 0] = rows_done[col, i * BS : (i + 1) * BS, :]
        for j in range(2):
            block = child[2 + i, 1 + j] - delta[i * BS : (i + 1) * BS, j * BS : (j + 1) * BS]
            out[2 + i, 1 + j] = block
            slices[pl.ds(2 * i + j, BS, stride=16), :] = block
    for i in range(2):
        for j in range(4):
            slices[pl.ds(8 + 4 * i + j, BS, stride=16), :] = parent[i, j]


def extend_add_kernel(maps, came, out, pivot_rows, panel_rows):
    for d in range(128):
        out[d * SLOTS : d * SLOTS + 8, :] = came[d * 16 + 8 : d * 16 + 16, :]
    for front in range(4):
        col_at = []
        for v in range(16):
            target = maps[front, v]
            col_at.append((target % 8) * SLOTS + target // 8)

        def one_row(u, carry):
            target = maps[front, u]
            row_at = (target % 16) * (8 * SLOTS) + (target // 16) * 4
            source = (front * 4 + u % 4) * (8 * 16) + (u // 4) * 2
            totals = []
            for v in range(16):
                totals.append(
                    out[pl.ds(row_at + col_at[v], 1), :]
                    + came[pl.ds(source + (v % 8) * 16 + v // 8, 1), :]
                )
            for v in range(16):
                out[pl.ds(row_at + col_at[v], 1), :] = totals[v]
            return carry

        lax.fori_loop(0, 16, one_row, 0)
    pivot_rows[...] = jnp.zeros_like(pivot_rows)
    panel_rows[...] = jnp.zeros_like(panel_rows)
    for q, (i, j) in enumerate(LOWER):
        at = (i * 8 + j) * SLOTS
        pivot_rows[q : q + 1, :] = out[at : at + 1, :]
    pivots = pivot_rows[...]
    for j in range(32):
        for k in range(KPB):
            at = ((j % 16) * 8 + k) * SLOTS + (j // 16) * 4
            panel_rows[j % 4, k : k + 1, :] = out[at : at + 1, :]
        for f in range(4):
            at = ((f * 4 + j // 8) * 8 + j % 8) * SLOTS
            out[at + 8 : at + 16, :] = panel_rows[j % 4]
            out[at + 16 : at + SLOTS, :] = pivots


def collect_kernel(came, own, rows, panel):
    for b in range(8):
        block = came[pl.ds(b, BS, stride=SLOTS), :]
        own[b // 4, b % 4] = block
        if b % 4 == 0:
            rows[b // 4] = block
    for b in range(KPB):
        panel[b] = came[pl.ds(8 + b, BS, stride=SLOTS), :]


def own_group():
    return lax.axis_index("front") * 4 + lax.axis_index("row")


def parent_pivots_kernel(
    came, lower_high, lower_low, inverse_high, inverse_low, own, work, upper, inverse, elements
):
    group, col = own_group(), own_col()
    for q, (i, j) in enumerate(LOWER):
        work[i * BS : (i + 1) * BS, j * BS : (j + 1) * BS] = came[pl.ds(16 + q, BS, stride=SLOTS), :]
    factor_pivots(
        KPB, work, upper, lower_high, lower_low, inverse, inverse_high, inverse_low, elements
    )
    row = jnp.minimum(group, KPB - 1)
    at = jnp.minimum(col, KPB - 1)
    block = work[pl.ds(pl.multiple_of(row * BS, BS), BS), pl.ds(pl.multiple_of(at * BS, BS), BS)]
    own[...] = jnp.where(row >= at, block, 0.0)


def parent_panels_kernel(
    lower_high, lower_low, inverse_high, inverse_low, rows_in, panel_0, panel_1, panel_2, panel_3, blocks, own,
    out, work, done, done_high, done_low
):
    group, col = own_group(), own_col()
    for k in range(KPB):
        here = slice(k * BS, (k + 1) * BS)
        for i in range(2):
            work[i * BS : (i + 1) * BS, here] = rows_in[k, i]
        for shift, panel in enumerate((panel_0, panel_1, panel_2, panel_3)):
            j = (lax.axis_index("row") + 4 - shift) % 4
            work[pl.ds(pl.multiple_of((2 + j) * BS, BS), BS), here] = panel[k]
    for k in range(KPB):
        here = slice(k * BS, (k + 1) * BS)
        solved = dot3(split(work[:, here]), (inverse_high[k], inverse_low[k]), NT)
        done[k] = solved[0 : 2 * BS, :]
        rows = split(solved)
        done_high[:, here] = rows[0]
        done_low[:, here] = rows[1]
        if k + 1 < KPB:
            below = slice((k + 1) * BS, KPB * BS)
            lower = (lower_high[below, here], lower_low[below, here])
            work[:, below] = work[:, below] - dot3(rows, lower, NT)
    left = (done_high[0 : 2 * BS, :], done_low[0 : 2 * BS, :])
    right = (done_high[2 * BS :, :], done_low[2 * BS :, :])
    delta = dot3(left, right, NT)
    at = jnp.minimum(col, KPB - 1)
    for i in range(2):
        row_pivot = group + 16 * i < KPB
        for j in range(4):
            col_pivot = col + 8 * j < KPB
            updated = blocks[i, j] - delta[i * BS : (i + 1) * BS, j * BS : (j + 1) * BS]
            if i == 0:
                updated = jnp.where(row_pivot, 0.0, updated)
            if j == 0:
                column = done[at, i * BS : (i + 1) * BS, :]
                if i == 0:
                    column = jnp.where(row_pivot, own[...], column)
                updated = jnp.where(col_pivot, column, updated)
            out[i, j] = updated


def call(kernel, outs, scratch, name, vmem, flops=0):
    def run(*args, smem=0):
        specs = [pl.BlockSpec(memory_space=pltpu.SMEM)] * smem
        specs += [pl.BlockSpec(memory_space=pltpu.VMEM)] * (len(args) - smem)
        size = sum(a.size * a.dtype.itemsize for a in args)
        return pl.pallas_call(
            kernel,
            out_shape=[jax.ShapeDtypeStruct(s, t) for s, t in outs],
            in_specs=specs,
            out_specs=[pl.BlockSpec(memory_space=pltpu.VMEM)] * len(outs),
            scratch_shapes=[pltpu.VMEM(s, t) for s, t in scratch],
            compiler_params=pltpu.CompilerParams(vmem_limit_bytes=vmem * MIB),
            cost_estimate=pl.CostEstimate(flops=flops, bytes_accessed=size, transcendentals=0),
            name=name,
        )(*args)

    return run


def pivots_call(kernel, pivots, own_shape, name):
    n = pivots * BS
    return call(
        kernel,
        [((n, n), BF16), ((n, n), BF16), ((pivots, BS, BS), BF16), ((pivots, BS, BS), BF16), (own_shape, F32)],
        [((n, n), F32), ((BS, BS), F32), ((BS, BS), F32), ((2, 8, 8, BS), F32)],
        name,
        24,
        flops=30_000_000_000,
    )


def shards(child_fronts, parent_front, child_maps):
    child = child_fronts.reshape(6, 3, BS, BS)
    parent = parent_front.reshape(2, 4, BS, BS)

    payload, rows_in, cols_in = call(
        prepare_kernel,
        [((16, BS + 8, BS), F32), ((4, BS, BS), F32), ((2, 2, BS, BS), F32)],
        [],
        "prepare",
        16,
    )(child)
    rows_in = lax.all_gather(rows_in, COL, axis=0)
    cols_in = lax.all_gather(cols_in, "row", axis=0)
    mine = lax.all_to_all(payload, ("row", "y"), 0, 0, tiled=True)
    other = lax.ppermute(mine, "core", [(0, 1), (1, 0)])

    factors = pivots_call(child_pivots_kernel, KCB, (2, BS, BS), "child_pivots")(mine, other)
    n = KCB * BS
    child_done, slices = call(
        child_panels_kernel,
        [((6, 3, BS, BS), F32), ((BS * 16, BS), F32)],
        [
            ((512, n), F32), ((n, 256), F32), ((KCB, 512, BS), F32),
            ((512, n), BF16), ((512, n), BF16), ((n, 256), BF16), ((n, 256), BF16),
        ],
        "child_panels",
        32,
        flops=3_000_000_000,
    )(*factors[:4], rows_in.reshape(KCB, 512, BS), cols_in, child, factors[4], parent)

    came = lax.all_to_all(slices.reshape(128, 16, BS), ALL, 0, 0, tiled=True)
    (sent,) = call(
        extend_add_kernel,
        [((128 * SLOTS, BS), F32)],
        [((24, BS), F32), ((4, 8, BS), F32)],
        "extend_add",
        16,
    )(child_maps, came.reshape(128 * 16, BS), smem=1)
    came = lax.all_to_all(sent.reshape(128, SLOTS, BS), ALL, 0, 0, tiled=True).reshape(128 * SLOTS, BS)
    blocks, rows_in, panel = call(
        collect_kernel,
        [((2, 4, BS, BS), F32), ((2, BS, BS), F32), ((KPB, BS, BS), F32)],
        [],
        "collect",
        16,
    )(came)
    rows_in = lax.all_gather(rows_in, COL, axis=0)
    panels = [panel] + [
        lax.ppermute(panel, "row", [(i, (i + shift) % 4) for i in range(4)]) for shift in (1, 2, 3)
    ]
    factors = pivots_call(parent_pivots_kernel, KPB, (BS, BS), "parent_pivots")(came)
    n = KPB * BS
    (parent_done,) = call(
        parent_panels_kernel,
        [((2, 4, BS, BS), F32)],
        [((n, n), F32), ((KPB, 256, BS), F32), ((n, n), BF16), ((n, n), BF16)],
        "parent_panels",
        24,
        flops=3_000_000_000,
    )(*factors[:4], rows_in, *panels, blocks, factors[4])
    return child_done.reshape(child_fronts.shape), parent_done.reshape(parent_front.shape)


def solution(mesh):
    mesh = jax.sharding.Mesh(mesh.devices.reshape(4, 4, 4, 2), ALL)
    child_spec = P("front", None, "row", None, COL, None, None)
    parent_spec = P(None, ("front", "row"), None, COL, None, None)
    return jax.shard_map(
        shards,
        mesh=mesh,
        in_specs=(child_spec, parent_spec, P()),
        out_specs=(child_spec, parent_spec),
        check_vma=False,
    )
```

```python
import functools

import jax
import jax.numpy as jnp
from jax import lax
from jax.experimental import pallas as pl
from jax.experimental.pallas import tpu as pltpu
from jax.sharding import PartitionSpec as P

BS = 128
KCB = 8
KPB = 6
F32 = jnp.float32
BF16 = jnp.bfloat16
COL = ("y", "core")
ALL = ("front", "row", "y", "core")
SLOTS = 40
LOWER = [(i, j) for i in range(KPB) for j in range(i + 1)]
MIB = 1024 * 1024


def split(x):
    high = x.astype(BF16)
    low = (x - high.astype(F32)).astype(BF16)
    return high, low


def dot3(a, b, dims):
    def one(x, y):
        return lax.dot_general(x, y, (dims, ((), ())), preferred_element_type=F32)

    left = jnp.concatenate(a, axis=dims[0][0])
    right = jnp.concatenate((b[0], b[0]), axis=dims[1][0])
    return one(left, right) + one(a[0], b[1])


NT = ((1,), (1,))
NN = ((1,), (0,))


def tree_sum(terms):
    terms = list(terms)
    while len(terms) > 1:
        terms = [sum(terms[i + 1 : i + 2], terms[i]) for i in range(0, len(terms), 2)]
    return terms[0]


def factor_block(load, store_upper, store_inverse, elements, between=lambda p: None):
    panels = BS // 8
    full = (8, BS)
    sub = lax.broadcasted_iota(jnp.int32, full, 0)
    lane = lax.broadcasted_iota(jnp.int32, full, 1)
    rest = [load(t) for t in range(panels)]
    inverse = [jnp.where(lane == sub + 8 * t, 1.0, 0.0).astype(F32) for t in range(panels)]
    for p in range(panels):
        at = 8 * p
        pivot_rows = rest[p]
        for i in range(8):
            elements[p % 2, i] = jnp.broadcast_to(pivot_rows[:, at + i : at + i + 1], full)
        e = {}
        for i in range(8):
            for k in range(i, 8):
                e[k, i] = jnp.broadcast_to(elements[p % 2, i, k : k + 1, :], full)
        c = {}
        for t in range(p + 1, panels):
            for i in range(8):
                c[t, i] = jnp.broadcast_to(rest[t][:, at + i : at + i + 1], full)
        unit, n, root, over = {}, {}, {}, {}
        for i in range(8):
            over[i] = pl.reciprocal(e[i, i])
            root[i] = lax.rsqrt(e[i, i])
            for k in range(i + 1, 8):
                unit[k, i] = e[k, i] * over[i]
                for j in range(i + 1, k + 1):
                    e[k, j] = e[k, j] - unit[k, i] * e[j, i]
            for k in range(i):
                total = unit[i, k]
                for m in range(k + 1, i):
                    total = total + unit[i, m] * n[m, k]
                n[i, k] = -total

        def forward(x):
            source = [jnp.broadcast_to(x[k : k + 1, :], full) for k in range(8)]
            solved = [tree_sum([n[i, k] * source[k] for k in range(i)] + [source[i]]) for i in range(8)]
            joined = solved[0] * root[0]
            for i in range(1, 8):
                joined = jnp.where(sub == i, solved[i] * root[i], joined)
            return solved, joined

        def backward(solved):
            scaled = [solved[i] * over[i] for i in range(8)]
            return [tree_sum([scaled[i]] + [n[k, i] * scaled[k] for k in range(i + 1, 8)]) for i in range(8)]

        upper_rows, upper = forward(pivot_rows)
        inverse_rows, inverse_out = forward(inverse[p])
        store_upper(p, jnp.where(lane >= sub + at, upper, 0.0))
        store_inverse(p, inverse_out)
        if p + 1 < panels:
            upper_rows = backward(upper_rows)
            inverse_rows = backward(inverse_rows)
            for t in range(p + 1, panels):
                rest[t] = rest[t] - tree_sum([c[t, i] * upper_rows[i] for i in range(8)])
                inverse[t] = inverse[t] - tree_sum([c[t, i] * inverse_rows[i] for i in range(8)])
        between(p)


def factor_pivots(
    pivots, work, upper, lower_high, lower_low, inverse, inverse_high, inverse_low, elements, waiting
):
    def blk(i, count=1):
        return slice(i * BS, (i + count) * BS)

    def panel(rows, here, inv):
        solved = dot3(split(work[rows, here]), inv, NT)
        work[rows, here] = solved
        high, low = split(solved)
        lower_high[rows, here] = high
        lower_low[rows, here] = low

    def update(rows, cols, here):
        left = (lower_high[rows, here], lower_low[rows, here])
        right = (lower_high[cols, here], lower_low[cols, here])
        work[rows, cols] = work[rows, cols] - dot3(left, right, NT)

    for k in range(pivots):
        here = blk(k)

        def load(t):
            return work[k * BS + 8 * t : k * BS + 8 * t + 8, here]

        def store_upper(t, x):
            upper[8 * t : 8 * t + 8, :] = x

        def store_inverse(t, x):
            inverse[8 * t : 8 * t + 8, :] = x

        share = -(-len(waiting) // 12)

        def between(p):
            for _ in range(share):
                if waiting:
                    waiting.pop(0)()

        factor_block(load, store_upper, store_inverse, elements, between)
        inv = split(inverse[...])
        inverse_high[k] = inv[0]
        inverse_low[k] = inv[1]
        if k + 1 < pivots:
            panel(blk(k + 1), here, inv)
            update(blk(k + 1), blk(k + 1), here)
        work[here, here] = jnp.transpose(upper[...])
        if k + 2 < pivots:
            after = slice((k + 2) * BS, pivots * BS)
            waiting.append(functools.partial(panel, after, here, inv))
            waiting.append(functools.partial(update, after, blk(k + 1), here))
            for j in range(k + 2, pivots, 2):
                wide = min(2, pivots - j)
                for i in range(j, pivots, 2):
                    tall = min(2, pivots - i)
                    waiting.append(functools.partial(update, blk(i, tall), blk(j, wide), here))


def own_col():
    return lax.axis_index("y") * 2 + lax.axis_index("core")


def prepare_kernel(child, payload, rows_out, cols_out):
    row, col = lax.axis_index("row"), own_col()
    half = BS // 2
    here = lax.broadcasted_iota(jnp.int32, (half, BS), 0)
    lane = lax.broadcasted_iota(jnp.int32, (half, BS), 1)
    for s in range(2):
        block = child[s, 0]
        at = row + 4 * s
        top, bottom = block[:half], block[half:]
        turned = jnp.transpose(block)[half:]
        packed = jnp.where((lane < half) | (lane - half > here), bottom, pltpu.roll(top, half, 1))
        sent = jnp.where(at > col, top, jnp.where(at < col, turned, packed))
        payload[0, s * half : (s + 1) * half, :] = sent
        diagonal = jnp.sum(jnp.where(lane - half == here, bottom, 0.0), axis=0, keepdims=True)

        @pl.when(at == col)
        def _():
            payload[0, BS : BS + 8, :] = jnp.broadcast_to(diagonal, (8, BS))

    @pl.when((row != col) & (row + 4 != col))
    def _():
        payload[0, BS : BS + 8, :] = jnp.zeros((8, BS), F32)

    for d in range(1, 16):
        payload[d] = payload[0]
    for i in range(4):
        for d in range(8):
            rows_out[d, i] = child[2 + i, 0]
    for i in range(2):
        for j in range(2):
            cols_out[i, j] = child[i, 1 + j]


def child_pivots_kernel(
    mine, other, lower_high, lower_low, inverse_high, inverse_low, own, work, upper, inverse, elements
):
    row, col, core = lax.axis_index("row"), own_col(), lax.axis_index("core")
    half = BS // 2
    here = lax.broadcasted_iota(jnp.int32, (half, BS), 0)
    lane = lax.broadcasted_iota(jnp.int32, (half, BS), 1)
    eye = lax.broadcasted_iota(jnp.int32, (BS, BS), 0) == lax.broadcasted_iota(jnp.int32, (BS, BS), 1)

    def received(i, j, rows):
        at = (i % 4) * 4 + j // 2
        return jnp.where(core == j % 2, mine[at, rows, :], other[at, rows, :])

    def piece(i, j):
        return received(i, j, slice((i // 4) * half, (i // 4 + 1) * half))

    def unpack(i):
        packed = piece(i, i)
        diagonal = received(i, i, slice(BS, BS + 1))
        at = slice(i * BS, (i + 1) * BS)
        work[i * BS : i * BS + half, at] = jnp.where(lane <= here, pltpu.roll(packed, half, 1), 0.0)
        work[i * BS + half : (i + 1) * BS, at] = jnp.where(
            (lane < half) | (lane - half > here), packed, jnp.where(lane - half == here, diagonal, 0.0)
        )
        part = work[at, at]
        work[at, at] = part + jnp.where(eye, 0.0, jnp.transpose(part))
        for j in range(i):
            work[i * BS : i * BS + half, j * BS : (j + 1) * BS] = piece(i, j)
            work[i * BS + half : (i + 1) * BS, j * BS : (j + 1) * BS] = piece(j, i)

    unpack(0)
    factor_pivots(
        KCB, work, upper, lower_high, lower_low, inverse, inverse_high, inverse_low, elements,
        [functools.partial(unpack, i) for i in range(1, KCB)],
    )
    for i in range(2):
        at = row + 4 * i
        block = work[pl.ds(pl.multiple_of(at * BS, BS), BS), pl.ds(pl.multiple_of(col * BS, BS), BS)]
        own[i] = jnp.where(at >= col, block, 0.0)


def bring(pairs, sems):
    copies = [pltpu.make_async_copy(a, b, sems.at[q]) for q, (a, b) in enumerate(pairs)]
    for copy in copies:
        copy.start()
    return copies


def below(k, pivots):
    return slice((k + 1) * BS, pivots * BS)


def child_panels_kernel(
    lower_high_at, lower_low_at, inverse_high_at, inverse_low_at, rows_at,
    cols_0, cols_1, cols_2, cols_3, child_at, own_at, parent_at,
    out, slices,
    lower_high, lower_low, inverse_high, inverse_low, rows_in, cols_in, child, own, parent,
    cols_work, rows_work, rows_done, rows_high, rows_low, cols_high, cols_low, sems
):
    col = own_col()
    first = [
        (inverse_high_at, inverse_high), (inverse_low_at, inverse_low), (rows_at, rows_in),
        (cols_0, cols_in.at[0]), (cols_1, cols_in.at[1]), (cols_2, cols_in.at[2]), (cols_3, cols_in.at[3]),
    ]
    for k in range(KCB - 1):
        at = (below(k, KCB), slice(k * BS, (k + 1) * BS))
        first += [(lower_high_at.at[at], lower_high.at[at]), (lower_low_at.at[at], lower_low.at[at])]
    copies = bring(first + [(child_at, child), (own_at, own), (parent_at, parent)], sems)
    for copy in copies[:7]:
        copy.wait()
    for shift in range(4):
        source = (lax.axis_index("row") + 4 - shift) % 4
        for i in range(2):
            for j in range(2):
                at = pl.ds(pl.multiple_of((4 * i + source) * BS, BS), BS)
                cols_work[at, j * BS : (j + 1) * BS] = cols_in[shift, i, j]
    for k in range(KCB):
        rows_work[:, k * BS : (k + 1) * BS] = rows_in[k]
    for k in range(KCB):
        here = slice(k * BS, (k + 1) * BS)
        inv = (inverse_high[k], inverse_low[k])
        solved = dot3(split(rows_work[:, here]), inv, NT)
        rows_done[k] = solved
        rows = split(solved)
        rows_high[:, here] = rows[0]
        rows_low[:, here] = rows[1]
        cols = split(dot3(inv, split(cols_work[here, :]), NN))
        cols_high[here, :] = cols[0]
        cols_low[here, :] = cols[1]
        if k + 1 < KCB:
            copies[7 + 2 * k].wait()
            copies[8 + 2 * k].wait()
            rest = below(k, KCB)
            lower = (lower_high[rest, here], lower_low[rest, here])
            rows_work[:, rest] = rows_work[:, rest] - dot3(rows, lower, NT)
            cols_work[rest, :] = cols_work[rest, :] - dot3(lower, cols, NN)
    for copy in copies[5 + 2 * KCB :]:
        copy.wait()
    delta = dot3((rows_high[...], rows_low[...]), (cols_high[...], cols_low[...]), NN)
    zero = jnp.zeros((BS, BS), F32)
    for i in range(2):
        out[i, 0] = own[i]
        for j in range(2):
            out[i, 1 + j] = zero
    for i in range(4):
        out[2 + i, 0] = rows_done[col, i * BS : (i + 1) * BS, :]
        for j in range(2):
            block = child[2 + i, 1 + j] - delta[i * BS : (i + 1) * BS, j * BS : (j + 1) * BS]
            out[2 + i, 1 + j] = block
            slices[pl.ds(2 * i + j, BS, stride=16), :] = block
    for i in range(2):
        for j in range(4):
            slices[pl.ds(8 + 4 * i + j, BS, stride=16), :] = parent[i, j]


def extend_add_kernel(maps, came, out, pivot_rows, panel_rows):
    for d in range(128):
        out[d * SLOTS : d * SLOTS + 8, :] = came[d * 16 + 8 : d * 16 + 16, :]
    for front in range(4):
        col_at = []
        for v in range(16):
            target = maps[front, v]
            col_at.append((target % 8) * SLOTS + target // 8)

        def one_row(u, carry):
            target = maps[front, u]
            row_at = (target % 16) * (8 * SLOTS) + (target // 16) * 4
            source = (front * 4 + u % 4) * (8 * 16) + (u // 4) * 2
            totals = []
            for v in range(16):
                totals.append(
                    out[pl.ds(row_at + col_at[v], 1), :]
                    + came[pl.ds(source + (v % 8) * 16 + v // 8, 1), :]
                )
            for v in range(16):
                out[pl.ds(row_at + col_at[v], 1), :] = totals[v]
            return carry

        lax.fori_loop(0, 16, one_row, 0)
    pivot_rows[...] = jnp.zeros_like(pivot_rows)
    panel_rows[...] = jnp.zeros_like(panel_rows)
    for q, (i, j) in enumerate(LOWER):
        at = (i * 8 + j) * SLOTS
        pivot_rows[q : q + 1, :] = out[at : at + 1, :]
    pivots = pivot_rows[...]
    for j in range(32):
        for k in range(KPB):
            at = ((j % 16) * 8 + k) * SLOTS + (j // 16) * 4
            panel_rows[j % 4, k : k + 1, :] = out[at : at + 1, :]
        for f in range(4):
            at = ((f * 4 + j // 8) * 8 + j % 8) * SLOTS
            out[at + 8 : at + 16, :] = panel_rows[j % 4]
            out[at + 16 : at + SLOTS, :] = pivots


def collect_kernel(came, own, rows, panel):
    for b in range(8):
        block = came[pl.ds(b, BS, stride=SLOTS), :]
        own[b // 4, b % 4] = block
        if b % 4 == 0:
            for d in range(8):
                rows[d, b // 4] = block
    for b in range(KPB):
        panel[b] = came[pl.ds(8 + b, BS, stride=SLOTS), :]


def own_group():
    return lax.axis_index("front") * 4 + lax.axis_index("row")


def parent_pivots_kernel(
    came, lower_high, lower_low, inverse_high, inverse_low, own, work, upper, inverse, elements
):
    group, col = own_group(), own_col()
    def unpack(q):
        i, j = LOWER[q]
        work[i * BS : (i + 1) * BS, j * BS : (j + 1) * BS] = came[pl.ds(16 + q, BS, stride=SLOTS), :]

    unpack(0)
    factor_pivots(
        KPB, work, upper, lower_high, lower_low, inverse, inverse_high, inverse_low, elements,
        [functools.partial(unpack, q) for q in range(1, len(LOWER))],
    )
    row = jnp.minimum(group, KPB - 1)
    at = jnp.minimum(col, KPB - 1)
    block = work[pl.ds(pl.multiple_of(row * BS, BS), BS), pl.ds(pl.multiple_of(at * BS, BS), BS)]
    own[...] = jnp.where(row >= at, block, 0.0)


def parent_panels_kernel(
    lower_high_at, lower_low_at, inverse_high_at, inverse_low_at, rows_at,
    panel_0, panel_1, panel_2, panel_3, blocks_at, own_at,
    out,
    lower_high, lower_low, inverse_high, inverse_low, rows_in, panels, blocks, own,
    work, done, done_high, done_low, sems
):
    group, col = own_group(), own_col()
    first = [
        (inverse_high_at, inverse_high), (inverse_low_at, inverse_low), (rows_at, rows_in),
        (panel_0, panels.at[0]), (panel_1, panels.at[1]), (panel_2, panels.at[2]), (panel_3, panels.at[3]),
    ]
    for k in range(KPB - 1):
        at = (below(k, KPB), slice(k * BS, (k + 1) * BS))
        first += [(lower_high_at.at[at], lower_high.at[at]), (lower_low_at.at[at], lower_low.at[at])]
    copies = bring(first + [(blocks_at, blocks), (own_at, own)], sems)
    for copy in copies[:7]:
        copy.wait()
    for k in range(KPB):
        here = slice(k * BS, (k + 1) * BS)
        for i in range(2):
            work[i * BS : (i + 1) * BS, here] = rows_in[k, i]
        for shift in range(4):
            j = (lax.axis_index("row") + 4 - shift) % 4
            work[pl.ds(pl.multiple_of((2 + j) * BS, BS), BS), here] = panels[shift, k]
    for k in range(KPB):
        here = slice(k * BS, (k + 1) * BS)
        solved = dot3(split(work[:, here]), (inverse_high[k], inverse_low[k]), NT)
        done[k] = solved[0 : 2 * BS, :]
        rows = split(solved)
        done_high[:, here] = rows[0]
        done_low[:, here] = rows[1]
        if k + 1 < KPB:
            copies[7 + 2 * k].wait()
            copies[8 + 2 * k].wait()
            rest = below(k, KPB)
            lower = (lower_high[rest, here], lower_low[rest, here])
            work[:, rest] = work[:, rest] - dot3(rows, lower, NT)
    for copy in copies[5 + 2 * KPB :]:
        copy.wait()
    left = (done_high[0 : 2 * BS, :], done_low[0 : 2 * BS, :])
    right = (done_high[2 * BS :, :], done_low[2 * BS :, :])
    delta = dot3(left, right, NT)
    at = jnp.minimum(col, KPB - 1)
    for i in range(2):
        row_pivot = group + 16 * i < KPB
        for j in range(4):
            col_pivot = col + 8 * j < KPB
            updated = blocks[i, j] - delta[i * BS : (i + 1) * BS, j * BS : (j + 1) * BS]
            if i == 0:
                updated = jnp.where(row_pivot, 0.0, updated)
            if j == 0:
                column = done[at, i * BS : (i + 1) * BS, :]
                if i == 0:
                    column = jnp.where(row_pivot, own[...], column)
                updated = jnp.where(col_pivot, column, updated)
            out[i, j] = updated


def call(kernel, outs, scratch, name, vmem, flops=0):
    def run(*args, smem=0, copies=0):
        specs = [pl.BlockSpec(memory_space=pltpu.SMEM)] * smem
        specs += [pl.BlockSpec(memory_space=pl.ANY if copies else pltpu.VMEM)] * (len(args) - smem)
        own_scratch = [pltpu.VMEM(s, t) for s, t in scratch]
        if copies:
            own_scratch.append(pltpu.SemaphoreType.DMA((copies,)))
        size = sum(a.size * a.dtype.itemsize for a in args)
        return pl.pallas_call(
            kernel,
            out_shape=[jax.ShapeDtypeStruct(s, t) for s, t in outs],
            in_specs=specs,
            out_specs=[pl.BlockSpec(memory_space=pltpu.VMEM)] * len(outs),
            scratch_shapes=own_scratch,
            compiler_params=pltpu.CompilerParams(vmem_limit_bytes=vmem * MIB),
            cost_estimate=pl.CostEstimate(flops=flops, bytes_accessed=size, transcendentals=0),
            name=name,
        )(*args)

    return run


def pivots_call(kernel, pivots, own_shape, name):
    n = pivots * BS
    return call(
        kernel,
        [((n, n), BF16), ((n, n), BF16), ((pivots, BS, BS), BF16), ((pivots, BS, BS), BF16), (own_shape, F32)],
        [((n, n), F32), ((BS, BS), F32), ((BS, BS), F32), ((2, 8, 8, BS), F32)],
        name,
        60,
        flops=30_000_000_000,
    )


def around(x, shift):
    return lax.ppermute(x, "row", [(i, (i + shift) % 4) for i in range(4)])


def shards(child_fronts, parent_front, child_maps):
    child = child_fronts.reshape(6, 3, BS, BS)
    parent = parent_front.reshape(2, 4, BS, BS)

    payload, rows_in, cols_in = call(
        prepare_kernel,
        [((16, BS + 8, BS), F32), ((8, 4, BS, BS), F32), ((2, 2, BS, BS), F32)],
        [],
        "prepare",
        60,
    )(child)
    mine = lax.all_to_all(payload, ("row", "y"), 0, 0, tiled=True)
    other = lax.ppermute(mine, "core", [(0, 1), (1, 0)])
    mine, other, rows_in, cols_in = lax.optimization_barrier((mine, other, rows_in, cols_in))
    rows_in = lax.all_to_all(rows_in, COL, 0, 0, tiled=True)
    cols_in = [cols_in] + [around(cols_in, shift) for shift in (1, 2, 3)]

    factors = pivots_call(child_pivots_kernel, KCB, (2, BS, BS), "child_pivots")(mine, other)
    n = KCB * BS
    child_done, slices = call(
        child_panels_kernel,
        [((6, 3, BS, BS), F32), ((BS * 16, BS), F32)],
        [
            ((n, n), BF16), ((n, n), BF16), ((KCB, BS, BS), BF16), ((KCB, BS, BS), BF16), ((KCB, 512, BS), F32),
            ((4, 2, 2, BS, BS), F32), ((6, 3, BS, BS), F32), ((2, BS, BS), F32), ((2, 4, BS, BS), F32),
            ((n, 256), F32), ((512, n), F32), ((KCB, 512, BS), F32),
            ((512, n), BF16), ((512, n), BF16), ((n, 256), BF16), ((n, 256), BF16),
        ],
        "child_panels",
        60,
        flops=3_000_000_000,
    )(*factors[:4], rows_in.reshape(KCB, 512, BS), *cols_in, child, factors[4], parent, copies=24)

    came = lax.all_to_all(slices.reshape(128, 16, BS), ALL, 0, 0, tiled=True)
    (sent,) = call(
        extend_add_kernel,
        [((128 * SLOTS, BS), F32)],
        [((24, BS), F32), ((4, 8, BS), F32)],
        "extend_add",
        16,
    )(child_maps, came.reshape(128 * 16, BS), smem=1)
    came = lax.all_to_all(sent.reshape(128, SLOTS, BS), ALL, 0, 0, tiled=True).reshape(128 * SLOTS, BS)
    blocks, rows_in, panel = call(
        collect_kernel,
        [((2, 4, BS, BS), F32), ((8, 2, BS, BS), F32), ((KPB, BS, BS), F32)],
        [],
        "collect",
        16,
    )(came)
    rows_in = lax.all_to_all(rows_in, COL, 0, 0, tiled=True)
    panels = [panel] + [around(panel, shift) for shift in (1, 2, 3)]
    factors = pivots_call(parent_pivots_kernel, KPB, (BS, BS), "parent_pivots")(came)
    n = KPB * BS
    (parent_done,) = call(
        parent_panels_kernel,
        [((2, 4, BS, BS), F32)],
        [
            ((n, n), BF16), ((n, n), BF16), ((KPB, BS, BS), BF16), ((KPB, BS, BS), BF16), ((8, 2, BS, BS), F32),
            ((4, KPB, BS, BS), F32), ((2, 4, BS, BS), F32), ((BS, BS), F32),
            ((n, n), F32), ((KPB, 256, BS), F32), ((n, n), BF16), ((n, n), BF16),
        ],
        "parent_panels",
        60,
        flops=3_000_000_000,
    )(*factors[:4], rows_in, *panels, blocks, factors[4], copies=19)
    return child_done.reshape(child_fronts.shape), parent_done.reshape(parent_front.shape)


def solution(mesh):
    mesh = jax.sharding.Mesh(mesh.devices.reshape(4, 4, 4, 2), ALL)
    child_spec = P("front", None, "row", None, COL, None, None)
    parent_spec = P(None, ("front", "row"), None, COL, None, None)
    return jax.shard_map(
        shards,
        mesh=mesh,
        in_specs=(child_spec, parent_spec, P()),
        out_specs=(child_spec, parent_spec),
        check_vma=False,
    )
```

```python
import functools

import jax
import jax.numpy as jnp
from jax import lax
from jax.experimental import pallas as pl
from jax.experimental.pallas import tpu as pltpu
from jax.sharding import PartitionSpec as P

BS = 128
KCB = 8
KPB = 6
F32 = jnp.float32
BF16 = jnp.bfloat16
COL = ("y", "core")
ALL = ("front", "row", "y", "core")
SLOTS = 24
PAIRS = [(2, 3), (4, 5)]
OFF = [(i, j) for i in range(1, KPB) for j in range(i)]
SHARE = 10
MIB = 1024 * 1024


def split(x):
    high = x.astype(BF16)
    low = (x - high.astype(F32)).astype(BF16)
    return high, low


def dot3(a, b, dims):
    def one(x, y):
        return lax.dot_general(x, y, (dims, ((), ())), preferred_element_type=F32)

    left = jnp.concatenate(a, axis=dims[0][0])
    right = jnp.concatenate((b[0], b[0]), axis=dims[1][0])
    return one(left, right) + one(a[0], b[1])


NT = ((1,), (1,))
NN = ((1,), (0,))


def tree_sum(terms):
    terms = list(terms)
    while len(terms) > 1:
        terms = [sum(terms[i + 1 : i + 2], terms[i]) for i in range(0, len(terms), 2)]
    return terms[0]


def factor_block(load, store_upper, store_inverse, elements, between=lambda p: None):
    panels = BS // 8
    full = (8, BS)
    sub = lax.broadcasted_iota(jnp.int32, full, 0)
    lane = lax.broadcasted_iota(jnp.int32, full, 1)
    rest = [load(t) for t in range(panels)]
    inverse = [jnp.where(lane == sub + 8 * t, 1.0, 0.0).astype(F32) for t in range(panels)]
    for p in range(panels):
        at = 8 * p
        pivot_rows = rest[p]
        for i in range(8):
            elements[p % 2, i] = jnp.broadcast_to(pivot_rows[:, at + i : at + i + 1], full)
        e = {}
        for i in range(8):
            for k in range(i, 8):
                e[k, i] = jnp.broadcast_to(elements[p % 2, i, k : k + 1, :], full)
        c = {}
        for t in range(p + 1, panels):
            for i in range(8):
                c[t, i] = jnp.broadcast_to(rest[t][:, at + i : at + i + 1], full)
        unit, n, root, over = {}, {}, {}, {}
        for i in range(8):
            over[i] = pl.reciprocal(e[i, i])
            root[i] = lax.rsqrt(e[i, i])
            for k in range(i + 1, 8):
                unit[k, i] = e[k, i] * over[i]
                for j in range(i + 1, k + 1):
                    e[k, j] = e[k, j] - unit[k, i] * e[j, i]
            for k in range(i):
                total = unit[i, k]
                for m in range(k + 1, i):
                    total = total + unit[i, m] * n[m, k]
                n[i, k] = -total

        def forward(x):
            source = [jnp.broadcast_to(x[k : k + 1, :], full) for k in range(8)]
            solved = [tree_sum([n[i, k] * source[k] for k in range(i)] + [source[i]]) for i in range(8)]
            joined = solved[0] * root[0]
            for i in range(1, 8):
                joined = jnp.where(sub == i, solved[i] * root[i], joined)
            return solved, joined

        def backward(solved):
            scaled = [solved[i] * over[i] for i in range(8)]
            return [tree_sum([scaled[i]] + [n[k, i] * scaled[k] for k in range(i + 1, 8)]) for i in range(8)]

        upper_rows, upper = forward(pivot_rows)
        inverse_rows, inverse_out = forward(inverse[p])
        store_upper(p, jnp.where(lane >= sub + at, upper, 0.0))
        store_inverse(p, inverse_out)
        if p + 1 < panels:
            upper_rows = backward(upper_rows)
            inverse_rows = backward(inverse_rows)
            for t in range(p + 1, panels):
                rest[t] = rest[t] - tree_sum([c[t, i] * upper_rows[i] for i in range(8)])
                inverse[t] = inverse[t] - tree_sum([c[t, i] * inverse_rows[i] for i in range(8)])
        between(p)


def factor_pivots(
    pivots, work, upper, lower_high, lower_low, inverse, inverse_high, inverse_low, elements, waiting
):
    def blk(i, count=1):
        return slice(i * BS, (i + count) * BS)

    def panel(rows, here, inv):
        solved = dot3(split(work[rows, here]), inv, NT)
        work[rows, here] = solved
        high, low = split(solved)
        lower_high[rows, here] = high
        lower_low[rows, here] = low

    def update(rows, cols, here):
        left = (lower_high[rows, here], lower_low[rows, here])
        right = (lower_high[cols, here], lower_low[cols, here])
        work[rows, cols] = work[rows, cols] - dot3(left, right, NT)

    for k in range(pivots):
        here = blk(k)

        def load(t):
            return work[k * BS + 8 * t : k * BS + 8 * t + 8, here]

        def store_upper(t, x):
            upper[8 * t : 8 * t + 8, :] = x

        def store_inverse(t, x):
            inverse[8 * t : 8 * t + 8, :] = x

        share = -(-len(waiting) // 12)

        def between(p):
            for _ in range(share):
                if waiting:
                    waiting.pop(0)()

        factor_block(load, store_upper, store_inverse, elements, between)
        inv = split(inverse[...])
        inverse_high[k] = inv[0]
        inverse_low[k] = inv[1]
        if k + 1 < pivots:
            panel(blk(k + 1), here, inv)
            update(blk(k + 1), blk(k + 1), here)
        work[here, here] = jnp.transpose(upper[...])
        if k + 2 < pivots:
            after = slice((k + 2) * BS, pivots * BS)
            waiting.append(functools.partial(panel, after, here, inv))
            waiting.append(functools.partial(update, after, blk(k + 1), here))
            for j in range(k + 2, pivots, 2):
                wide = min(2, pivots - j)
                for i in range(j, pivots, 2):
                    tall = min(2, pivots - i)
                    waiting.append(functools.partial(update, blk(i, tall), blk(j, wide), here))


def own_col():
    return lax.axis_index("y") * 2 + lax.axis_index("core")


def prepare_kernel(child, payload, rows_out, cols_out):
    row, col = lax.axis_index("row"), own_col()
    half = BS // 2
    here = lax.broadcasted_iota(jnp.int32, (half, BS), 0)
    lane = lax.broadcasted_iota(jnp.int32, (half, BS), 1)
    for s in range(2):
        block = child[s, 0]
        at = row + 4 * s
        top, bottom = block[:half], block[half:]
        turned = jnp.transpose(block)[half:]
        packed = jnp.where((lane < half) | (lane - half > here), bottom, pltpu.roll(top, half, 1))
        sent = jnp.where(at > col, top, jnp.where(at < col, turned, packed))
        payload[0, s * half : (s + 1) * half, :] = sent
        diagonal = jnp.sum(jnp.where(lane - half == here, bottom, 0.0), axis=0, keepdims=True)

        @pl.when(at == col)
        def _():
            payload[0, BS : BS + 8, :] = jnp.broadcast_to(diagonal, (8, BS))

    @pl.when((row != col) & (row + 4 != col))
    def _():
        payload[0, BS : BS + 8, :] = jnp.zeros((8, BS), F32)

    for d in range(1, 16):
        payload[d] = payload[0]
    for i in range(4):
        for d in range(8):
            rows_out[d, i] = child[2 + i, 0]
    for i in range(2):
        for j in range(2):
            cols_out[i, j] = child[i, 1 + j]


def child_pivots_kernel(
    mine, other, lower_high, lower_low, inverse_high, inverse_low, own, work, upper, inverse, elements
):
    row, col, core = lax.axis_index("row"), own_col(), lax.axis_index("core")
    half = BS // 2
    here = lax.broadcasted_iota(jnp.int32, (half, BS), 0)
    lane = lax.broadcasted_iota(jnp.int32, (half, BS), 1)
    eye = lax.broadcasted_iota(jnp.int32, (BS, BS), 0) == lax.broadcasted_iota(jnp.int32, (BS, BS), 1)

    def received(i, j, rows):
        at = (i % 4) * 4 + j // 2
        return jnp.where(core == j % 2, mine[at, rows, :], other[at, rows, :])

    def piece(i, j):
        return received(i, j, slice((i // 4) * half, (i // 4 + 1) * half))

    def unpack(i):
        packed = piece(i, i)
        diagonal = received(i, i, slice(BS, BS + 1))
        at = slice(i * BS, (i + 1) * BS)
        work[i * BS : i * BS + half, at] = jnp.where(lane <= here, pltpu.roll(packed, half, 1), 0.0)
        work[i * BS + half : (i + 1) * BS, at] = jnp.where(
            (lane < half) | (lane - half > here), packed, jnp.where(lane - half == here, diagonal, 0.0)
        )
        part = work[at, at]
        work[at, at] = part + jnp.where(eye, 0.0, jnp.transpose(part))
        for j in range(i):
            work[i * BS : i * BS + half, j * BS : (j + 1) * BS] = piece(i, j)
            work[i * BS + half : (i + 1) * BS, j * BS : (j + 1) * BS] = piece(j, i)

    unpack(0)
    factor_pivots(
        KCB, work, upper, lower_high, lower_low, inverse, inverse_high, inverse_low, elements,
        [functools.partial(unpack, i) for i in range(1, KCB)],
    )
    for i in range(2):
        at = row + 4 * i
        block = work[pl.ds(pl.multiple_of(at * BS, BS), BS), pl.ds(pl.multiple_of(col * BS, BS), BS)]
        own[i] = jnp.where(at >= col, block, 0.0)


def bring(pairs, sems):
    copies = [pltpu.make_async_copy(a, b, sems.at[q]) for q, (a, b) in enumerate(pairs)]
    for copy in copies:
        copy.start()
    return copies


def child_panels_kernel(
    lower_high_at, lower_low_at, inverse_high_at, inverse_low_at, rows_at,
    cols_0, cols_1, cols_2, cols_3, child_at, own_at, parent_at,
    out, slices,
    lower_high, lower_low, inverse_high, inverse_low, rows_in, cols_in, child, own, parent,
    cols_work, rows_done, rows_high, rows_low, cols_high, cols_low, sems
):
    col = own_col()
    first = [
        (inverse_high_at, inverse_high), (inverse_low_at, inverse_low), (rows_at, rows_in),
        (cols_0, cols_in.at[0]), (cols_1, cols_in.at[1]), (cols_2, cols_in.at[2]), (cols_3, cols_in.at[3]),
    ]
    for k in range(1, KCB):
        at = (slice(k * BS, (k + 1) * BS), slice(0, k * BS))
        first += [(lower_high_at.at[at], lower_high.at[at]), (lower_low_at.at[at], lower_low.at[at])]
    copies = bring(first + [(child_at, child), (own_at, own), (parent_at, parent)], sems)
    for copy in copies[:7]:
        copy.wait()
    for shift in range(4):
        source = (lax.axis_index("row") + 4 - shift) % 4
        for i in range(2):
            for j in range(2):
                at = pl.ds(pl.multiple_of((4 * i + source) * BS, BS), BS)
                cols_work[at, j * BS : (j + 1) * BS] = cols_in[shift, i, j]
    for k in range(KCB):
        here = slice(k * BS, (k + 1) * BS)
        rows, cols = rows_in[k], cols_work[here, :]
        if k:
            copies[5 + 2 * k].wait()
            copies[6 + 2 * k].wait()
            past = slice(0, k * BS)
            lower = (lower_high[here, past], lower_low[here, past])
            rows = rows - dot3((rows_high[:, past], rows_low[:, past]), lower, NT)
            cols = cols - dot3(lower, (cols_high[past, :], cols_low[past, :]), NN)
        inv = (inverse_high[k], inverse_low[k])
        solved = dot3(split(rows), inv, NT)
        rows_done[k] = solved
        rows_high[:, here], rows_low[:, here] = split(solved)
        cols_high[here, :], cols_low[here, :] = split(dot3(inv, split(cols), NN))
    for copy in copies[5 + 2 * KCB :]:
        copy.wait()
    delta = dot3((rows_high[...], rows_low[...]), (cols_high[...], cols_low[...]), NN)
    zero = jnp.zeros((BS, BS), F32)
    for i in range(2):
        out[i, 0] = own[i]
        for j in range(2):
            out[i, 1 + j] = zero
    for i in range(4):
        out[2 + i, 0] = rows_done[col, i * BS : (i + 1) * BS, :]
        for j in range(2):
            block = child[2 + i, 1 + j] - delta[i * BS : (i + 1) * BS, j * BS : (j + 1) * BS]
            out[2 + i, 1 + j] = block
            slices[pl.ds(2 * i + j, BS, stride=16), :] = block
    for i in range(2):
        for j in range(4):
            slices[pl.ds(8 + 4 * i + j, BS, stride=16), :] = parent[i, j]


def extend_add_kernel(maps, came, out, panel_rows):
    for d in range(128):
        out[d * SLOTS : d * SLOTS + 8, :] = came[d * 16 + 8 : d * 16 + 16, :]
    for front in range(4):
        col_at = []
        for v in range(16):
            target = maps[front, v]
            col_at.append((target % 8) * SLOTS + target // 8)

        def one_row(u, carry):
            target = maps[front, u]
            row_at = (target % 16) * (8 * SLOTS) + (target // 16) * 4
            source = (front * 4 + u % 4) * (8 * 16) + (u // 4) * 2
            totals = []
            for v in range(16):
                totals.append(
                    out[pl.ds(row_at + col_at[v], 1), :]
                    + came[pl.ds(source + (v % 8) * 16 + v // 8, 1), :]
                )
            for v in range(16):
                out[pl.ds(row_at + col_at[v], 1), :] = totals[v]
            return carry

        lax.fori_loop(0, 16, one_row, 0)
    lane = lax.broadcasted_iota(jnp.int32, (1, BS), 1)
    own_at = lax.axis_index(ALL)

    def block_row(i, j):
        at = (i * 8 + j) * SLOTS
        return out[at : at + 1, :]

    rows = [block_row(0, 0), block_row(1, 1)]
    diagonals = jnp.zeros((1, BS), F32)
    for q, (i, j) in enumerate(PAIRS):
        second = block_row(j, j)
        rows.append(jnp.where(lane <= own_at, block_row(i, i), second))
        value = jnp.sum(jnp.where(lane == own_at, second, 0.0), axis=1, keepdims=True)
        diagonals = jnp.where(lane == q, value, diagonals)
    rows.append(diagonals)
    rows += [block_row(i, j) for i, j in OFF]
    for q, x in enumerate(rows):
        for half in (q // SHARE, q // SHARE + 2):
            at = KPB + q % SHARE
            panel_rows[half, at : at + 1, :] = x
    for j in range(32):
        for k in range(KPB):
            at = ((j % 16) * 8 + k) * SLOTS + (j // 16) * 4
            panel_rows[j % 4, k : k + 1, :] = out[at : at + 1, :]
        for f in range(4):
            at = ((f * 4 + j // 8) * 8 + j % 8) * SLOTS
            out[at + 8 : at + SLOTS, :] = panel_rows[j % 4]


def collect_kernel(came, own, rows, panel, pivots):
    for b in range(8):
        block = came[pl.ds(b, BS, stride=SLOTS), :]
        own[b // 4, b % 4] = block
        if b % 4 == 0:
            for d in range(8):
                rows[d, b // 4] = block
    for b in range(KPB):
        panel[b] = came[pl.ds(8 + b, BS, stride=SLOTS), :]
    for b in range(SHARE):
        pivots[b] = came[pl.ds(8 + KPB + b, BS, stride=SLOTS), :]


def own_group():
    return lax.axis_index("front") * 4 + lax.axis_index("row")


def parent_pivots_kernel(
    mine, other, lower_high, lower_low, inverse_high, inverse_low, own, work, upper, inverse, elements
):
    group, col = own_group(), own_col()
    core = lax.axis_index("core")
    here = lax.broadcasted_iota(jnp.int32, (BS, BS), 0)
    lane = lax.broadcasted_iota(jnp.int32, (BS, BS), 1)

    def received(q):
        return jnp.where(core == q // SHARE, mine[q % SHARE], other[q % SHARE])

    def place(i, j, x):
        work[i * BS : (i + 1) * BS, j * BS : (j + 1) * BS] = x

    def unpack(q, i, j):
        place(i, j, received(q))

    def unpack_lower(q, i):
        x = received(q)
        place(i, i, jnp.where(here >= lane, x, 0.0) + jnp.transpose(jnp.where(here > lane, x, 0.0)))

    def unpack_upper(q, i):
        x = jnp.where(here < lane, received(2 + q), 0.0)
        at = slice(q, q + 1)
        diagonal = jnp.where(core == 4 // SHARE, mine[4 % SHARE, :, at], other[4 % SHARE, :, at])
        place(i, i, x + jnp.transpose(x) + jnp.where(here == lane, diagonal, 0.0))

    unpack(0, 0, 0)
    waiting = [functools.partial(unpack, 5 + q, i, j) for q, (i, j) in enumerate(OFF)]
    waiting.append(functools.partial(unpack, 1, 1, 1))
    for q, (i, j) in enumerate(PAIRS):
        waiting.append(functools.partial(unpack_lower, 2 + q, i))
        waiting.append(functools.partial(unpack_upper, q, j))
    factor_pivots(
        KPB, work, upper, lower_high, lower_low, inverse, inverse_high, inverse_low, elements, waiting
    )
    row = jnp.minimum(group, KPB - 1)
    at = jnp.minimum(col, KPB - 1)
    block = work[pl.ds(pl.multiple_of(row * BS, BS), BS), pl.ds(pl.multiple_of(at * BS, BS), BS)]
    own[...] = jnp.where(row >= at, block, 0.0)


def parent_panels_kernel(
    lower_high_at, lower_low_at, inverse_high_at, inverse_low_at, rows_at,
    panel_0, panel_1, panel_2, panel_3, blocks_at, own_at,
    out,
    lower_high, lower_low, inverse_high, inverse_low, rows_in, panels, blocks, own,
    work, done, done_high, done_low, sems
):
    group, col = own_group(), own_col()
    first = [
        (inverse_high_at, inverse_high), (inverse_low_at, inverse_low), (rows_at, rows_in),
        (panel_0, panels.at[0]), (panel_1, panels.at[1]), (panel_2, panels.at[2]), (panel_3, panels.at[3]),
    ]
    for k in range(1, KPB):
        at = (slice(k * BS, (k + 1) * BS), slice(0, k * BS))
        first += [(lower_high_at.at[at], lower_high.at[at]), (lower_low_at.at[at], lower_low.at[at])]
    copies = bring(first + [(blocks_at, blocks), (own_at, own)], sems)
    for copy in copies[:7]:
        copy.wait()
    for k in range(KPB):
        here = slice(k * BS, (k + 1) * BS)
        for i in range(2):
            work[i * BS : (i + 1) * BS, here] = rows_in[k, i]
        for shift in range(4):
            j = (lax.axis_index("row") + 4 - shift) % 4
            work[pl.ds(pl.multiple_of((2 + j) * BS, BS), BS), here] = panels[shift, k]
    for k in range(KPB):
        here = slice(k * BS, (k + 1) * BS)
        rows = work[:, here]
        if k:
            copies[5 + 2 * k].wait()
            copies[6 + 2 * k].wait()
            past = slice(0, k * BS)
            lower = (lower_high[here, past], lower_low[here, past])
            rows = rows - dot3((done_high[:, past], done_low[:, past]), lower, NT)
        solved = dot3(split(rows), (inverse_high[k], inverse_low[k]), NT)
        done[k] = solved[0 : 2 * BS, :]
        done_high[:, here], done_low[:, here] = split(solved)
    for copy in copies[5 + 2 * KPB :]:
        copy.wait()
    left = (done_high[0 : 2 * BS, :], done_low[0 : 2 * BS, :])
    right = (done_high[2 * BS :, :], done_low[2 * BS :, :])
    delta = dot3(left, right, NT)
    at = jnp.minimum(col, KPB - 1)
    for i in range(2):
        row_pivot = group + 16 * i < KPB
        for j in range(4):
            col_pivot = col + 8 * j < KPB
            updated = blocks[i, j] - delta[i * BS : (i + 1) * BS, j * BS : (j + 1) * BS]
            if i == 0:
                updated = jnp.where(row_pivot, 0.0, updated)
            if j == 0:
                column = done[at, i * BS : (i + 1) * BS, :]
                if i == 0:
                    column = jnp.where(row_pivot, own[...], column)
                updated = jnp.where(col_pivot, column, updated)
            out[i, j] = updated


def call(kernel, outs, scratch, name, vmem, flops=0):
    def run(*args, smem=0, copies=0):
        specs = [pl.BlockSpec(memory_space=pltpu.SMEM)] * smem
        specs += [pl.BlockSpec(memory_space=pl.ANY if copies else pltpu.VMEM)] * (len(args) - smem)
        own_scratch = [pltpu.VMEM(s, t) for s, t in scratch]
        if copies:
            own_scratch.append(pltpu.SemaphoreType.DMA((copies,)))
        size = sum(a.size * a.dtype.itemsize for a in args)
        return pl.pallas_call(
            kernel,
            out_shape=[jax.ShapeDtypeStruct(s, t) for s, t in outs],
            in_specs=specs,
            out_specs=[pl.BlockSpec(memory_space=pltpu.VMEM)] * len(outs),
            scratch_shapes=own_scratch,
            compiler_params=pltpu.CompilerParams(vmem_limit_bytes=vmem * MIB),
            cost_estimate=pl.CostEstimate(flops=flops, bytes_accessed=size, transcendentals=0),
            name=name,
        )(*args)

    return run


def pivots_call(kernel, pivots, own_shape, name):
    n = pivots * BS
    return call(
        kernel,
        [((n, n), BF16), ((n, n), BF16), ((pivots, BS, BS), BF16), ((pivots, BS, BS), BF16), (own_shape, F32)],
        [((n, n), F32), ((BS, BS), F32), ((BS, BS), F32), ((2, 8, 8, BS), F32)],
        name,
        60,
        flops=30_000_000_000,
    )


def swap(x):
    return lax.ppermute(x, "core", [(0, 1), (1, 0)])


def around(x, shift):
    return lax.ppermute(x, "row", [(i, (i + shift) % 4) for i in range(4)])


def shards(child_fronts, parent_front, child_maps):
    child = child_fronts.reshape(6, 3, BS, BS)
    parent = parent_front.reshape(2, 4, BS, BS)

    payload, rows_in, cols_in = call(
        prepare_kernel,
        [((16, BS + 8, BS), F32), ((8, 4, BS, BS), F32), ((2, 2, BS, BS), F32)],
        [],
        "prepare",
        60,
    )(child)
    mine = lax.all_to_all(payload, ("row", "y"), 0, 0, tiled=True)
    other = swap(mine)
    mine, other, rows_in, cols_in = lax.optimization_barrier((mine, other, rows_in, cols_in))
    rows_in = lax.all_to_all(rows_in, COL, 0, 0, tiled=True)
    cols_in = [cols_in] + [around(cols_in, shift) for shift in (1, 2, 3)]

    factors = pivots_call(child_pivots_kernel, KCB, (2, BS, BS), "child_pivots")(mine, other)
    n = KCB * BS
    child_done, slices = call(
        child_panels_kernel,
        [((6, 3, BS, BS), F32), ((BS * 16, BS), F32)],
        [
            ((n, n), BF16), ((n, n), BF16), ((KCB, BS, BS), BF16), ((KCB, BS, BS), BF16), ((KCB, 512, BS), F32),
            ((4, 2, 2, BS, BS), F32), ((6, 3, BS, BS), F32), ((2, BS, BS), F32), ((2, 4, BS, BS), F32),
            ((n, 256), F32), ((KCB, 512, BS), F32),
            ((512, n), BF16), ((512, n), BF16), ((n, 256), BF16), ((n, 256), BF16),
        ],
        "child_panels",
        60,
        flops=3_000_000_000,
    )(*factors[:4], rows_in.reshape(KCB, 512, BS), *cols_in, child, factors[4], parent, copies=24)

    came = lax.all_to_all(slices.reshape(128, 16, BS), ALL, 0, 0, tiled=True)
    (sent,) = call(
        extend_add_kernel,
        [((128 * SLOTS, BS), F32)],
        [((4, KPB + SHARE, BS), F32)],
        "extend_add",
        16,
    )(child_maps, came.reshape(128 * 16, BS), smem=1)
    came = lax.all_to_all(sent.reshape(128, SLOTS, BS), ALL, 0, 0, tiled=True).reshape(128 * SLOTS, BS)
    blocks, rows_in, panel, mine = call(
        collect_kernel,
        [((2, 4, BS, BS), F32), ((8, 2, BS, BS), F32), ((KPB, BS, BS), F32), ((SHARE, BS, BS), F32)],
        [],
        "collect",
        16,
    )(came)
    other = swap(mine)
    rows_in = lax.all_to_all(rows_in, COL, 0, 0, tiled=True)
    panels = [panel] + [around(panel, shift) for shift in (1, 2, 3)]
    factors = pivots_call(parent_pivots_kernel, KPB, (BS, BS), "parent_pivots")(mine, other)
    n = KPB * BS
    (parent_done,) = call(
        parent_panels_kernel,
        [((2, 4, BS, BS), F32)],
        [
            ((n, n), BF16), ((n, n), BF16), ((KPB, BS, BS), BF16), ((KPB, BS, BS), BF16), ((8, 2, BS, BS), F32),
            ((4, KPB, BS, BS), F32), ((2, 4, BS, BS), F32), ((BS, BS), F32),
            ((n, n), F32), ((KPB, 256, BS), F32), ((n, n), BF16), ((n, n), BF16),
        ],
        "parent_panels",
        60,
        flops=3_000_000_000,
    )(*factors[:4], rows_in, *panels, blocks, factors[4], copies=19)
    return child_done.reshape(child_fronts.shape), parent_done.reshape(parent_front.shape)


def solution(mesh):
    mesh = jax.sharding.Mesh(mesh.devices.reshape(4, 4, 4, 2), ALL)
    child_spec = P("front", None, "row", None, COL, None, None)
    parent_spec = P(None, ("front", "row"), None, COL, None, None)
    return jax.shard_map(
        shards,
        mesh=mesh,
        in_specs=(child_spec, parent_spec, P()),
        out_specs=(child_spec, parent_spec),
        check_vma=False,
    )
```

```python
import functools

import jax
import jax.numpy as jnp
from jax import lax
from jax.experimental import pallas as pl
from jax.experimental.pallas import tpu as pltpu
from jax.sharding import PartitionSpec as P

BS = 128
KCB = 8
KPB = 6
F32 = jnp.float32
BF16 = jnp.bfloat16
COL = ("y", "core")
ALL = ("front", "row", "y", "core")
SLOTS = 24
PAIRS = [(2, 3), (4, 5)]
OFF = [(i, j) for i in range(1, KPB) for j in range(i)]
SHARE = 10
MIB = 1024 * 1024


def split(x):
    high = x.astype(BF16)
    low = (x - high.astype(F32)).astype(BF16)
    return high, low


def dot3(a, b, dims):
    def one(x, y):
        return lax.dot_general(x, y, (dims, ((), ())), preferred_element_type=F32)

    left = jnp.concatenate(a, axis=dims[0][0])
    right = jnp.concatenate((b[0], b[0]), axis=dims[1][0])
    return one(left, right) + one(a[0], b[1])


NT = ((1,), (1,))
NN = ((1,), (0,))


def tree_sum(terms):
    terms = list(terms)
    while len(terms) > 1:
        terms = [sum(terms[i + 1 : i + 2], terms[i]) for i in range(0, len(terms), 2)]
    return terms[0]


def factor_block(load, store_upper, store_inverse, elements, between=lambda p: None):
    panels = BS // 8
    full = (8, BS)
    sub = lax.broadcasted_iota(jnp.int32, full, 0)
    lane = lax.broadcasted_iota(jnp.int32, full, 1)
    rest = [load(t) for t in range(panels)]
    inverse = [jnp.where(lane == sub + 8 * t, 1.0, 0.0).astype(F32) for t in range(panels)]
    for p in range(panels):
        at = 8 * p
        pivot_rows = rest[p]
        for i in range(8):
            elements[p % 2, i] = jnp.broadcast_to(pivot_rows[:, at + i : at + i + 1], full)
        e = {}
        for i in range(8):
            for k in range(i, 8):
                e[k, i] = jnp.broadcast_to(elements[p % 2, i, k : k + 1, :], full)
        c = {}
        for t in range(p + 1, panels):
            for i in range(8):
                c[t, i] = jnp.broadcast_to(rest[t][:, at + i : at + i + 1], full)
        unit, n, root, over = {}, {}, {}, {}
        for i in range(8):
            over[i] = pl.reciprocal(e[i, i])
            root[i] = lax.rsqrt(e[i, i])
            for k in range(i + 1, 8):
                unit[k, i] = e[k, i] * over[i]
                for j in range(i + 1, k + 1):
                    e[k, j] = e[k, j] - unit[k, i] * e[j, i]
            for k in range(i):
                total = unit[i, k]
                for m in range(k + 1, i):
                    total = total + unit[i, m] * n[m, k]
                n[i, k] = -total

        def forward(x):
            source = [jnp.broadcast_to(x[k : k + 1, :], full) for k in range(8)]
            solved = [tree_sum([n[i, k] * source[k] for k in range(i)] + [source[i]]) for i in range(8)]
            joined = solved[0] * root[0]
            for i in range(1, 8):
                joined = jnp.where(sub == i, solved[i] * root[i], joined)
            return solved, joined

        def backward(solved):
            scaled = [solved[i] * over[i] for i in range(8)]
            return [tree_sum([scaled[i]] + [n[k, i] * scaled[k] for k in range(i + 1, 8)]) for i in range(8)]

        upper_rows, upper = forward(pivot_rows)
        inverse_rows, inverse_out = forward(inverse[p])
        store_upper(p, jnp.where(lane >= sub + at, upper, 0.0))
        store_inverse(p, inverse_out)
        if p + 1 < panels:
            upper_rows = backward(upper_rows)
            inverse_rows = backward(inverse_rows)
            for t in range(p + 1, panels):
                rest[t] = rest[t] - tree_sum([c[t, i] * upper_rows[i] for i in range(8)])
                inverse[t] = inverse[t] - tree_sum([c[t, i] * inverse_rows[i] for i in range(8)])
        between(p)


def factor_pivots(
    pivots, work, upper, lower_high, lower_low, inverse, inverse_high, inverse_low, elements, waiting
):
    def blk(i, count=1):
        return slice(i * BS, (i + count) * BS)

    def panel(rows, here, inv):
        solved = dot3(split(work[rows, here]), inv, NT)
        work[rows, here] = solved
        high, low = split(solved)
        lower_high[rows, here] = high
        lower_low[rows, here] = low

    def update(rows, cols, here):
        left = (lower_high[rows, here], lower_low[rows, here])
        right = (lower_high[cols, here], lower_low[cols, here])
        work[rows, cols] = work[rows, cols] - dot3(left, right, NT)

    for k in range(pivots):
        here = blk(k)

        def load(t):
            return work[k * BS + 8 * t : k * BS + 8 * t + 8, here]

        def store_upper(t, x):
            upper[8 * t : 8 * t + 8, :] = x

        def store_inverse(t, x):
            inverse[8 * t : 8 * t + 8, :] = x

        share = -(-len(waiting) // 12)

        def between(p):
            for _ in range(share):
                if waiting:
                    waiting.pop(0)()

        factor_block(load, store_upper, store_inverse, elements, between)
        inv = split(inverse[...])
        inverse_high[k] = inv[0]
        inverse_low[k] = inv[1]
        if k + 1 < pivots:
            panel(blk(k + 1), here, inv)
            update(blk(k + 1), blk(k + 1), here)
        work[here, here] = jnp.transpose(upper[...])
        if k + 2 < pivots:
            after = slice((k + 2) * BS, pivots * BS)
            waiting.append(functools.partial(panel, after, here, inv))
            waiting.append(functools.partial(update, after, blk(k + 1), here))
            for j in range(k + 2, pivots, 2):
                wide = min(2, pivots - j)
                for i in range(j, pivots, 2):
                    tall = min(2, pivots - i)
                    waiting.append(functools.partial(update, blk(i, tall), blk(j, wide), here))


def own_col():
    return lax.axis_index("y") * 2 + lax.axis_index("core")


def prepare_kernel(child, payload, rows_out, cols_out):
    row, col = lax.axis_index("row"), own_col()
    half = BS // 2
    here = lax.broadcasted_iota(jnp.int32, (half, BS), 0)
    lane = lax.broadcasted_iota(jnp.int32, (half, BS), 1)
    for s in range(2):
        block = child[s, 0]
        at = row + 4 * s
        top, bottom = block[:half], block[half:]
        turned = jnp.transpose(block)[half:]
        packed = jnp.where((lane < half) | (lane - half > here), bottom, pltpu.roll(top, half, 1))
        sent = jnp.where(at > col, top, jnp.where(at < col, turned, packed))
        payload[0, s * half : (s + 1) * half, :] = sent
        diagonal = jnp.sum(jnp.where(lane - half == here, bottom, 0.0), axis=0, keepdims=True)

        @pl.when(at == col)
        def _():
            payload[0, BS : BS + 8, :] = jnp.broadcast_to(diagonal, (8, BS))

    @pl.when((row != col) & (row + 4 != col))
    def _():
        payload[0, BS : BS + 8, :] = jnp.zeros((8, BS), F32)

    for d in range(1, 16):
        payload[d] = payload[0]
    for i in range(4):
        for d in range(8):
            rows_out[d, i] = child[2 + i, 0]
    for i in range(2):
        for j in range(2):
            cols_out[i, j] = child[i, 1 + j]


def child_pivots_kernel(
    mine, other, lower_high, lower_low, inverse_high, inverse_low, own, work, upper, inverse, elements
):
    row, col, core = lax.axis_index("row"), own_col(), lax.axis_index("core")
    half = BS // 2
    here = lax.broadcasted_iota(jnp.int32, (half, BS), 0)
    lane = lax.broadcasted_iota(jnp.int32, (half, BS), 1)
    eye = lax.broadcasted_iota(jnp.int32, (BS, BS), 0) == lax.broadcasted_iota(jnp.int32, (BS, BS), 1)

    def received(i, j, rows):
        at = (i % 4) * 4 + j // 2
        return jnp.where(core == j % 2, mine[at, rows, :], other[at, rows, :])

    def piece(i, j):
        return received(i, j, slice((i // 4) * half, (i // 4 + 1) * half))

    def unpack(i):
        packed = piece(i, i)
        diagonal = received(i, i, slice(BS, BS + 1))
        at = slice(i * BS, (i + 1) * BS)
        work[i * BS : i * BS + half, at] = jnp.where(lane <= here, pltpu.roll(packed, half, 1), 0.0)
        work[i * BS + half : (i + 1) * BS, at] = jnp.where(
            (lane < half) | (lane - half > here), packed, jnp.where(lane - half == here, diagonal, 0.0)
        )
        part = work[at, at]
        work[at, at] = part + jnp.where(eye, 0.0, jnp.transpose(part))
        for j in range(i):
            work[i * BS : i * BS + half, j * BS : (j + 1) * BS] = piece(i, j)
            work[i * BS + half : (i + 1) * BS, j * BS : (j + 1) * BS] = piece(j, i)

    unpack(0)
    factor_pivots(
        KCB, work, upper, lower_high, lower_low, inverse, inverse_high, inverse_low, elements,
        [functools.partial(unpack, i) for i in range(1, KCB)],
    )
    for i in range(2):
        at = row + 4 * i
        block = work[pl.ds(pl.multiple_of(at * BS, BS), BS), pl.ds(pl.multiple_of(col * BS, BS), BS)]
        own[i] = jnp.where(at >= col, block, 0.0)


def bring(pairs, sems):
    copies = [pltpu.make_async_copy(a, b, sems.at[q]) for q, (a, b) in enumerate(pairs)]
    for copy in copies:
        copy.start()
    return copies


def below(k, pivots):
    return slice((k + 1) * BS, pivots * BS)


def child_panels_kernel(
    lower_high_at, lower_low_at, inverse_high_at, inverse_low_at, rows_at,
    cols_0, cols_1, cols_2, cols_3, child_at, own_at, parent_at,
    out, slices,
    lower_high, lower_low, inverse_high, inverse_low, rows_in, cols_in, child, own, parent,
    cols_work, rows_work, rows_done, rows_high, rows_low, cols_high, cols_low, sems
):
    col = own_col()
    first = [
        (inverse_high_at, inverse_high), (inverse_low_at, inverse_low), (rows_at, rows_in),
        (cols_0, cols_in.at[0]), (cols_1, cols_in.at[1]), (cols_2, cols_in.at[2]), (cols_3, cols_in.at[3]),
    ]
    for k in range(KCB - 1):
        at = (below(k, KCB), slice(k * BS, (k + 1) * BS))
        first += [(lower_high_at.at[at], lower_high.at[at]), (lower_low_at.at[at], lower_low.at[at])]
    copies = bring(first + [(child_at, child), (own_at, own), (parent_at, parent)], sems)
    for copy in copies[:7]:
        copy.wait()
    for shift in range(4):
        source = (lax.axis_index("row") + 4 - shift) % 4
        for i in range(2):
            for j in range(2):
                at = pl.ds(pl.multiple_of((4 * i + source) * BS, BS), BS)
                cols_work[at, j * BS : (j + 1) * BS] = cols_in[shift, i, j]
    for k in range(KCB):
        rows_work[:, k * BS : (k + 1) * BS] = rows_in[k]
    for k in range(KCB):
        here = slice(k * BS, (k + 1) * BS)
        inv = (inverse_high[k], inverse_low[k])
        solved = dot3(split(rows_work[:, here]), inv, NT)
        rows_done[k] = solved
        rows = split(solved)
        rows_high[:, here] = rows[0]
        rows_low[:, here] = rows[1]
        cols = split(dot3(inv, split(cols_work[here, :]), NN))
        cols_high[here, :] = cols[0]
        cols_low[here, :] = cols[1]
        if k + 1 < KCB:
            copies[7 + 2 * k].wait()
            copies[8 + 2 * k].wait()
            rest = below(k, KCB)
            lower = (lower_high[rest, here], lower_low[rest, here])
            rows_work[:, rest] = rows_work[:, rest] - dot3(rows, lower, NT)
            cols_work[rest, :] = cols_work[rest, :] - dot3(lower, cols, NN)
    for copy in copies[5 + 2 * KCB :]:
        copy.wait()
    delta = dot3((rows_high[...], rows_low[...]), (cols_high[...], cols_low[...]), NN)
    zero = jnp.zeros((BS, BS), F32)
    for i in range(2):
        out[i, 0] = own[i]
        for j in range(2):
            out[i, 1 + j] = zero
    for i in range(4):
        out[2 + i, 0] = rows_done[col, i * BS : (i + 1) * BS, :]
        for j in range(2):
            block = child[2 + i, 1 + j] - delta[i * BS : (i + 1) * BS, j * BS : (j + 1) * BS]
            out[2 + i, 1 + j] = block
            slices[pl.ds(2 * i + j, BS, stride=16), :] = block
    for i in range(2):
        for j in range(4):
            slices[pl.ds(8 + 4 * i + j, BS, stride=16), :] = parent[i, j]


def extend_add_kernel(maps, came, out, panel_rows):
    for d in range(128):
        out[d * SLOTS : d * SLOTS + 8, :] = came[d * 16 + 8 : d * 16 + 16, :]
    for front in range(4):
        col_at = []
        for v in range(16):
            target = maps[front, v]
            col_at.append((target % 8) * SLOTS + target // 8)

        def one_row(u, carry):
            target = maps[front, u]
            row_at = (target % 16) * (8 * SLOTS) + (target // 16) * 4
            source = (front * 4 + u % 4) * (8 * 16) + (u // 4) * 2
            totals = []
            for v in range(16):
                totals.append(
                    out[pl.ds(row_at + col_at[v], 1), :]
                    + came[pl.ds(source + (v % 8) * 16 + v // 8, 1), :]
                )
            for v in range(16):
                out[pl.ds(row_at + col_at[v], 1), :] = totals[v]
            return carry

        lax.fori_loop(0, 16, one_row, 0)
    lane = lax.broadcasted_iota(jnp.int32, (1, BS), 1)
    own_at = lax.axis_index(ALL)

    def block_row(i, j):
        at = (i * 8 + j) * SLOTS
        return out[at : at + 1, :]

    rows = [block_row(0, 0), block_row(1, 1)]
    diagonals = jnp.zeros((1, BS), F32)
    for q, (i, j) in enumerate(PAIRS):
        second = block_row(j, j)
        rows.append(jnp.where(lane <= own_at, block_row(i, i), second))
        value = jnp.sum(jnp.where(lane == own_at, second, 0.0), axis=1, keepdims=True)
        diagonals = jnp.where(lane == q, value, diagonals)
    rows.append(diagonals)
    rows += [block_row(i, j) for i, j in OFF]
    for q, x in enumerate(rows):
        for half in (q // SHARE, q // SHARE + 2):
            at = KPB + q % SHARE
            panel_rows[half, at : at + 1, :] = x
    for j in range(32):
        for k in range(KPB):
            at = ((j % 16) * 8 + k) * SLOTS + (j // 16) * 4
            panel_rows[j % 4, k : k + 1, :] = out[at : at + 1, :]
        for f in range(4):
            at = ((f * 4 + j // 8) * 8 + j % 8) * SLOTS
            out[at + 8 : at + SLOTS, :] = panel_rows[j % 4]


def collect_kernel(came, own, rows, panel, pivots):
    for b in range(8):
        block = came[pl.ds(b, BS, stride=SLOTS), :]
        own[b // 4, b % 4] = block
        if b % 4 == 0:
            for d in range(8):
                rows[d, b // 4] = block
    for b in range(KPB):
        panel[b] = came[pl.ds(8 + b, BS, stride=SLOTS), :]
    for b in range(SHARE):
        pivots[b] = came[pl.ds(8 + KPB + b, BS, stride=SLOTS), :]


def own_group():
    return lax.axis_index("front") * 4 + lax.axis_index("row")


def parent_pivots_kernel(
    mine, other, lower_high, lower_low, inverse_high, inverse_low, own, work, upper, inverse, elements
):
    group, col = own_group(), own_col()
    core = lax.axis_index("core")
    here = lax.broadcasted_iota(jnp.int32, (BS, BS), 0)
    lane = lax.broadcasted_iota(jnp.int32, (BS, BS), 1)

    def received(q):
        return jnp.where(core == q // SHARE, mine[q % SHARE], other[q % SHARE])

    def place(i, j, x):
        work[i * BS : (i + 1) * BS, j * BS : (j + 1) * BS] = x

    def unpack(q, i, j):
        place(i, j, received(q))

    def unpack_lower(q, i):
        x = received(q)
        place(i, i, jnp.where(here >= lane, x, 0.0) + jnp.transpose(jnp.where(here > lane, x, 0.0)))

    def unpack_upper(q, i):
        x = jnp.where(here < lane, received(2 + q), 0.0)
        at = slice(q, q + 1)
        diagonal = jnp.where(core == 4 // SHARE, mine[4 % SHARE, :, at], other[4 % SHARE, :, at])
        place(i, i, x + jnp.transpose(x) + jnp.where(here == lane, diagonal, 0.0))

    unpack(0, 0, 0)
    waiting = [functools.partial(unpack, 5 + q, i, j) for q, (i, j) in enumerate(OFF)]
    waiting.append(functools.partial(unpack, 1, 1, 1))
    for q, (i, j) in enumerate(PAIRS):
        waiting.append(functools.partial(unpack_lower, 2 + q, i))
        waiting.append(functools.partial(unpack_upper, q, j))
    factor_pivots(
        KPB, work, upper, lower_high, lower_low, inverse, inverse_high, inverse_low, elements, waiting
    )
    row = jnp.minimum(group, KPB - 1)
    at = jnp.minimum(col, KPB - 1)
    block = work[pl.ds(pl.multiple_of(row * BS, BS), BS), pl.ds(pl.multiple_of(at * BS, BS), BS)]
    own[...] = jnp.where(row >= at, block, 0.0)


def parent_panels_kernel(
    lower_high_at, lower_low_at, inverse_high_at, inverse_low_at, rows_at,
    panel_0, panel_1, panel_2, panel_3, blocks_at, own_at,
    out,
    lower_high, lower_low, inverse_high, inverse_low, rows_in, panels, blocks, own,
    work, done, done_high, done_low, sems
):
    group, col = own_group(), own_col()
    first = [
        (inverse_high_at, inverse_high), (inverse_low_at, inverse_low), (rows_at, rows_in),
        (panel_0, panels.at[0]), (panel_1, panels.at[1]), (panel_2, panels.at[2]), (panel_3, panels.at[3]),
    ]
    for k in range(KPB - 1):
        at = (below(k, KPB), slice(k * BS, (k + 1) * BS))
        first += [(lower_high_at.at[at], lower_high.at[at]), (lower_low_at.at[at], lower_low.at[at])]
    copies = bring(first + [(blocks_at, blocks), (own_at, own)], sems)
    for copy in copies[:7]:
        copy.wait()
    for k in range(KPB):
        here = slice(k * BS, (k + 1) * BS)
        for i in range(2):
            work[i * BS : (i + 1) * BS, here] = rows_in[k, i]
        for shift in range(4):
            j = (lax.axis_index("row") + 4 - shift) % 4
            work[pl.ds(pl.multiple_of((2 + j) * BS, BS), BS), here] = panels[shift, k]
    for k in range(KPB):
        here = slice(k * BS, (k + 1) * BS)
        solved = dot3(split(work[:, here]), (inverse_high[k], inverse_low[k]), NT)
        done[k] = solved[0 : 2 * BS, :]
        rows = split(solved)
        done_high[:, here] = rows[0]
        done_low[:, here] = rows[1]
        if k + 1 < KPB:
            copies[7 + 2 * k].wait()
            copies[8 + 2 * k].wait()
            rest = below(k, KPB)
            lower = (lower_high[rest, here], lower_low[rest, here])
            work[:, rest] = work[:, rest] - dot3(rows, lower, NT)
    for copy in copies[5 + 2 * KPB :]:
        copy.wait()
    left = (done_high[0 : 2 * BS, :], done_low[0 : 2 * BS, :])
    right = (done_high[2 * BS :, :], done_low[2 * BS :, :])
    delta = dot3(left, right, NT)
    at = jnp.minimum(col, KPB - 1)
    for i in range(2):
        row_pivot = group + 16 * i < KPB
        for j in range(4):
            col_pivot = col + 8 * j < KPB
            updated = blocks[i, j] - delta[i * BS : (i + 1) * BS, j * BS : (j + 1) * BS]
            if i == 0:
                updated = jnp.where(row_pivot, 0.0, updated)
            if j == 0:
                column = done[at, i * BS : (i + 1) * BS, :]
                if i == 0:
                    column = jnp.where(row_pivot, own[...], column)
                updated = jnp.where(col_pivot, column, updated)
            out[i, j] = updated


def call(kernel, outs, scratch, name, vmem, flops=0):
    def run(*args, smem=0, copies=0):
        specs = [pl.BlockSpec(memory_space=pltpu.SMEM)] * smem
        specs += [pl.BlockSpec(memory_space=pl.ANY if copies else pltpu.VMEM)] * (len(args) - smem)
        own_scratch = [pltpu.VMEM(s, t) for s, t in scratch]
        if copies:
            own_scratch.append(pltpu.SemaphoreType.DMA((copies,)))
        size = sum(a.size * a.dtype.itemsize for a in args)
        return pl.pallas_call(
            kernel,
            out_shape=[jax.ShapeDtypeStruct(s, t) for s, t in outs],
            in_specs=specs,
            out_specs=[pl.BlockSpec(memory_space=pltpu.VMEM)] * len(outs),
            scratch_shapes=own_scratch,
            compiler_params=pltpu.CompilerParams(vmem_limit_bytes=vmem * MIB),
            cost_estimate=pl.CostEstimate(flops=flops, bytes_accessed=size, transcendentals=0),
            name=name,
        )(*args)

    return run


def pivots_call(kernel, pivots, own_shape, name):
    n = pivots * BS
    return call(
        kernel,
        [((n, n), BF16), ((n, n), BF16), ((pivots, BS, BS), BF16), ((pivots, BS, BS), BF16), (own_shape, F32)],
        [((n, n), F32), ((BS, BS), F32), ((BS, BS), F32), ((2, 8, 8, BS), F32)],
        name,
        60,
        flops=30_000_000_000,
    )


def swap(x):
    return lax.ppermute(x, "core", [(0, 1), (1, 0)])


def around(x, shift):
    return lax.ppermute(x, "row", [(i, (i + shift) % 4) for i in range(4)])


def shards(child_fronts, parent_front, child_maps):
    child = child_fronts.reshape(6, 3, BS, BS)
    parent = parent_front.reshape(2, 4, BS, BS)

    payload, rows_in, cols_in = call(
        prepare_kernel,
        [((16, BS + 8, BS), F32), ((8, 4, BS, BS), F32), ((2, 2, BS, BS), F32)],
        [],
        "prepare",
        60,
    )(child)
    mine = lax.all_to_all(payload, ("row", "y"), 0, 0, tiled=True)
    other = swap(mine)
    mine, other, rows_in, cols_in = lax.optimization_barrier((mine, other, rows_in, cols_in))
    rows_in = lax.all_to_all(rows_in, COL, 0, 0, tiled=True)
    cols_in = [cols_in] + [around(cols_in, shift) for shift in (1, 2, 3)]

    factors = pivots_call(child_pivots_kernel, KCB, (2, BS, BS), "child_pivots")(mine, other)
    n = KCB * BS
    child_done, slices = call(
        child_panels_kernel,
        [((6, 3, BS, BS), F32), ((BS * 16, BS), F32)],
        [
            ((n, n), BF16), ((n, n), BF16), ((KCB, BS, BS), BF16), ((KCB, BS, BS), BF16), ((KCB, 512, BS), F32),
            ((4, 2, 2, BS, BS), F32), ((6, 3, BS, BS), F32), ((2, BS, BS), F32), ((2, 4, BS, BS), F32),
            ((n, 256), F32), ((512, n), F32), ((KCB, 512, BS), F32),
            ((512, n), BF16), ((512, n), BF16), ((n, 256), BF16), ((n, 256), BF16),
        ],
        "child_panels",
        60,
        flops=3_000_000_000,
    )(*factors[:4], rows_in.reshape(KCB, 512, BS), *cols_in, child, factors[4], parent, copies=24)

    came = lax.all_to_all(slices.reshape(128, 16, BS), ALL, 0, 0, tiled=True)
    (sent,) = call(
        extend_add_kernel,
        [((128 * SLOTS, BS), F32)],
        [((4, KPB + SHARE, BS), F32)],
        "extend_add",
        16,
    )(child_maps, came.reshape(128 * 16, BS), smem=1)
    came = lax.all_to_all(sent.reshape(128, SLOTS, BS), ALL, 0, 0, tiled=True).reshape(128 * SLOTS, BS)
    blocks, rows_in, panel, mine = call(
        collect_kernel,
        [((2, 4, BS, BS), F32), ((8, 2, BS, BS), F32), ((KPB, BS, BS), F32), ((SHARE, BS, BS), F32)],
        [],
        "collect",
        16,
    )(came)
    other = swap(mine)
    rows_in = lax.all_to_all(rows_in, COL, 0, 0, tiled=True)
    panels = [panel] + [around(panel, shift) for shift in (1, 2, 3)]
    factors = pivots_call(parent_pivots_kernel, KPB, (BS, BS), "parent_pivots")(mine, other)
    n = KPB * BS
    (parent_done,) = call(
        parent_panels_kernel,
        [((2, 4, BS, BS), F32)],
        [
            ((n, n), BF16), ((n, n), BF16), ((KPB, BS, BS), BF16), ((KPB, BS, BS), BF16), ((8, 2, BS, BS), F32),
            ((4, KPB, BS, BS), F32), ((2, 4, BS, BS), F32), ((BS, BS), F32),
            ((n, n), F32), ((KPB, 256, BS), F32), ((n, n), BF16), ((n, n), BF16),
        ],
        "parent_panels",
        60,
        flops=3_000_000_000,
    )(*factors[:4], rows_in, *panels, blocks, factors[4], copies=19)
    return child_done.reshape(child_fronts.shape), parent_done.reshape(parent_front.shape)


def solution(mesh):
    mesh = jax.sharding.Mesh(mesh.devices.reshape(4, 4, 4, 2), ALL)
    child_spec = P("front", None, "row", None, COL, None, None)
    parent_spec = P(None, ("front", "row"), None, COL, None, None)
    return jax.shard_map(
        shards,
        mesh=mesh,
        in_specs=(child_spec, parent_spec, P()),
        out_specs=(child_spec, parent_spec),
        check_vma=False,
    )
```

```python
import functools

import jax
import jax.numpy as jnp
from jax import lax
from jax.experimental import pallas as pl
from jax.experimental.pallas import tpu as pltpu
from jax.sharding import PartitionSpec as P

BS = 128
KCB = 8
KPB = 6
F32 = jnp.float32
BF16 = jnp.bfloat16
COL = ("y", "core")
ALL = ("front", "row", "y", "core")
SLOTS = 24
PAIRS = [(2, 3), (4, 5)]
OFF = [(i, j) for i in range(1, KPB) for j in range(i)]
SHARE = 10
MIB = 1024 * 1024


def split(x):
    high = x.astype(BF16)
    low = (x - high.astype(F32)).astype(BF16)
    return high, low


def dot3(a, b, dims):
    def one(x, y):
        return lax.dot_general(x, y, (dims, ((), ())), preferred_element_type=F32)

    left = jnp.concatenate(a, axis=dims[0][0])
    right = jnp.concatenate((b[0], b[0]), axis=dims[1][0])
    return one(left, right) + one(a[0], b[1])


NT = ((1,), (1,))
NN = ((1,), (0,))


def tree_sum(terms):
    terms = list(terms)
    while len(terms) > 1:
        terms = [sum(terms[i + 1 : i + 2], terms[i]) for i in range(0, len(terms), 2)]
    return terms[0]


def factor_block(load, store_upper, store_inverse, elements, between=lambda p: None):
    panels = BS // 8
    full = (8, BS)
    sub = lax.broadcasted_iota(jnp.int32, full, 0)
    lane = lax.broadcasted_iota(jnp.int32, full, 1)
    rest = [load(t) for t in range(panels)]
    inverse = [jnp.where(lane == sub + 8 * t, 1.0, 0.0).astype(F32) for t in range(panels)]
    for p in range(panels):
        at = 8 * p
        pivot_rows = rest[p]
        for i in range(8):
            elements[p % 2, i] = jnp.broadcast_to(pivot_rows[:, at + i : at + i + 1], full)
        e = {}
        for i in range(8):
            for k in range(i, 8):
                e[k, i] = jnp.broadcast_to(elements[p % 2, i, k : k + 1, :], full)
        c = {}
        for t in range(p + 1, panels):
            for i in range(8):
                c[t, i] = jnp.broadcast_to(rest[t][:, at + i : at + i + 1], full)
        unit, n, root, over = {}, {}, {}, {}
        for i in range(8):
            over[i] = pl.reciprocal(e[i, i])
            root[i] = lax.rsqrt(e[i, i])
            for k in range(i + 1, 8):
                unit[k, i] = e[k, i] * over[i]
                for j in range(i + 1, k + 1):
                    e[k, j] = e[k, j] - unit[k, i] * e[j, i]
            for k in range(i):
                total = unit[i, k]
                for m in range(k + 1, i):
                    total = total + unit[i, m] * n[m, k]
                n[i, k] = -total

        def forward(x):
            source = [jnp.broadcast_to(x[k : k + 1, :], full) for k in range(8)]
            solved = [tree_sum([n[i, k] * source[k] for k in range(i)] + [source[i]]) for i in range(8)]
            joined = solved[0] * root[0]
            for i in range(1, 8):
                joined = jnp.where(sub == i, solved[i] * root[i], joined)
            return solved, joined

        def backward(solved):
            scaled = [solved[i] * over[i] for i in range(8)]
            return [tree_sum([scaled[i]] + [n[k, i] * scaled[k] for k in range(i + 1, 8)]) for i in range(8)]

        upper_rows, upper = forward(pivot_rows)
        inverse_rows, inverse_out = forward(inverse[p])
        store_upper(p, jnp.where(lane >= sub + at, upper, 0.0))
        store_inverse(p, inverse_out)
        if p + 1 < panels:
            upper_rows = backward(upper_rows)
            inverse_rows = backward(inverse_rows)
            for t in range(p + 1, panels):
                rest[t] = rest[t] - tree_sum([c[t, i] * upper_rows[i] for i in range(8)])
                inverse[t] = inverse[t] - tree_sum([c[t, i] * inverse_rows[i] for i in range(8)])
        between(p)


def factor_pivots(
    pivots, work, upper, lower_high, lower_low, inverse, inverse_high, inverse_low, elements, waiting
):
    def blk(i, count=1):
        return slice(i * BS, (i + count) * BS)

    def panel(rows, here, inv):
        solved = dot3(split(work[rows, here]), inv, NT)
        work[rows, here] = solved
        high, low = split(solved)
        lower_high[rows, here] = high
        lower_low[rows, here] = low

    def update(rows, cols, here):
        left = (lower_high[rows, here], lower_low[rows, here])
        right = (lower_high[cols, here], lower_low[cols, here])
        work[rows, cols] = work[rows, cols] - dot3(left, right, NT)

    for k in range(pivots):
        here = blk(k)

        def load(t):
            return work[k * BS + 8 * t : k * BS + 8 * t + 8, here]

        def store_upper(t, x):
            upper[8 * t : 8 * t + 8, :] = x

        def store_inverse(t, x):
            inverse[8 * t : 8 * t + 8, :] = x

        share = -(-len(waiting) // 12)

        def between(p):
            for _ in range(share):
                if waiting:
                    waiting.pop(0)()

        factor_block(load, store_upper, store_inverse, elements, between)
        inv = split(inverse[...])
        inverse_high[k] = inv[0]
        inverse_low[k] = inv[1]
        if k + 1 < pivots:
            panel(blk(k + 1), here, inv)
            update(blk(k + 1), blk(k + 1), here)
        work[here, here] = jnp.transpose(upper[...])
        if k + 2 < pivots:
            after = slice((k + 2) * BS, pivots * BS)
            waiting.append(functools.partial(panel, after, here, inv))
            waiting.append(functools.partial(update, after, blk(k + 1), here))
            for j in range(k + 2, pivots, 2):
                wide = min(2, pivots - j)
                for i in range(j, pivots, 2):
                    tall = min(2, pivots - i)
                    waiting.append(functools.partial(update, blk(i, tall), blk(j, wide), here))


def own_col():
    return lax.axis_index("y") * 2 + lax.axis_index("core")


def prepare_kernel(child, payload, rows_out, cols_out):
    row, col = lax.axis_index("row"), own_col()
    half = BS // 2
    here = lax.broadcasted_iota(jnp.int32, (half, BS), 0)
    lane = lax.broadcasted_iota(jnp.int32, (half, BS), 1)
    for s in range(2):
        block = child[s, 0]
        at = row + 4 * s
        top, bottom = block[:half], block[half:]
        turned = jnp.transpose(block)[half:]
        packed = jnp.where((lane < half) | (lane - half > here), bottom, pltpu.roll(top, half, 1))
        sent = jnp.where(at > col, top, jnp.where(at < col, turned, packed))
        payload[0, s * half : (s + 1) * half, :] = sent
        diagonal = jnp.sum(jnp.where(lane - half == here, bottom, 0.0), axis=0, keepdims=True)

        @pl.when(at == col)
        def _():
            payload[0, BS : BS + 8, :] = jnp.broadcast_to(diagonal, (8, BS))

    @pl.when((row != col) & (row + 4 != col))
    def _():
        payload[0, BS : BS + 8, :] = jnp.zeros((8, BS), F32)

    for d in range(1, 16):
        payload[d] = payload[0]
    for i in range(4):
        for d in range(8):
            rows_out[d, i] = child[2 + i, 0]
    for i in range(2):
        for j in range(2):
            cols_out[i, j] = child[i, 1 + j]


def child_pivots_kernel(
    mine, other, lower_high, lower_low, inverse_high, inverse_low, own, work, upper, inverse, elements
):
    row, col, core = lax.axis_index("row"), own_col(), lax.axis_index("core")
    half = BS // 2
    here = lax.broadcasted_iota(jnp.int32, (half, BS), 0)
    lane = lax.broadcasted_iota(jnp.int32, (half, BS), 1)
    eye = lax.broadcasted_iota(jnp.int32, (BS, BS), 0) == lax.broadcasted_iota(jnp.int32, (BS, BS), 1)

    def received(i, j, rows):
        at = (i % 4) * 4 + j // 2
        return jnp.where(core == j % 2, mine[at, rows, :], other[at, rows, :])

    def piece(i, j):
        return received(i, j, slice((i // 4) * half, (i // 4 + 1) * half))

    def unpack(i):
        packed = piece(i, i)
        diagonal = received(i, i, slice(BS, BS + 1))
        at = slice(i * BS, (i + 1) * BS)
        work[i * BS : i * BS + half, at] = jnp.where(lane <= here, pltpu.roll(packed, half, 1), 0.0)
        work[i * BS + half : (i + 1) * BS, at] = jnp.where(
            (lane < half) | (lane - half > here), packed, jnp.where(lane - half == here, diagonal, 0.0)
        )
        part = work[at, at]
        work[at, at] = part + jnp.where(eye, 0.0, jnp.transpose(part))
        for j in range(i):
            work[i * BS : i * BS + half, j * BS : (j + 1) * BS] = piece(i, j)
            work[i * BS + half : (i + 1) * BS, j * BS : (j + 1) * BS] = piece(j, i)

    unpack(0)
    factor_pivots(
        KCB, work, upper, lower_high, lower_low, inverse, inverse_high, inverse_low, elements,
        [functools.partial(unpack, i) for i in range(1, KCB)],
    )
    for i in range(2):
        at = row + 4 * i
        block = work[pl.ds(pl.multiple_of(at * BS, BS), BS), pl.ds(pl.multiple_of(col * BS, BS), BS)]
        own[i] = jnp.where(at >= col, block, 0.0)


def bring(pairs, sems):
    copies = [pltpu.make_async_copy(a, b, sems.at[q]) for q, (a, b) in enumerate(pairs)]
    for copy in copies:
        copy.start()
    return copies


def below(k, pivots):
    return slice((k + 1) * BS, pivots * BS)


def child_panels_kernel(
    lower_high_at, lower_low_at, inverse_high_at, inverse_low_at, rows_at,
    cols_0, cols_1, cols_2, cols_3, child_at, own_at, parent_at,
    out, slices,
    lower_high, lower_low, inverse_high, inverse_low, cols_in, child, own, parent,
    cols_work, rows_work, rows_done, rows_high, rows_low, cols_high, cols_low, sems
):
    col = own_col()
    first = [
        (inverse_high_at, inverse_high), (inverse_low_at, inverse_low),
        (cols_0, cols_in.at[0]), (cols_1, cols_in.at[1]), (cols_2, cols_in.at[2]), (cols_3, cols_in.at[3]),
    ]
    first += [(rows_at.at[k], rows_work.at[:, k * BS : (k + 1) * BS]) for k in range(KCB)]
    for k in range(KCB - 1):
        at = (below(k, KCB), slice(k * BS, (k + 1) * BS))
        first += [(lower_high_at.at[at], lower_high.at[at]), (lower_low_at.at[at], lower_low.at[at])]
    copies = bring(first + [(child_at, child), (own_at, own), (parent_at, parent)], sems)
    for copy in copies[:14]:
        copy.wait()
    for shift in range(4):
        source = (lax.axis_index("row") + 4 - shift) % 4
        for i in range(2):
            for j in range(2):
                at = pl.ds(pl.multiple_of((4 * i + source) * BS, BS), BS)
                cols_work[at, j * BS : (j + 1) * BS] = cols_in[shift, i, j]
    for k in range(KCB):
        here = slice(k * BS, (k + 1) * BS)
        inv = (inverse_high[k], inverse_low[k])
        solved = dot3(split(rows_work[:, here]), inv, NT)
        rows_done[k] = solved
        rows = split(solved)
        rows_high[:, here] = rows[0]
        rows_low[:, here] = rows[1]
        cols = split(dot3(inv, split(cols_work[here, :]), NN))
        cols_high[here, :] = cols[0]
        cols_low[here, :] = cols[1]
        if k + 1 < KCB:
            copies[14 + 2 * k].wait()
            copies[15 + 2 * k].wait()
            rest = below(k, KCB)
            lower = (lower_high[rest, here], lower_low[rest, here])
            rows_work[:, rest] = rows_work[:, rest] - dot3(rows, lower, NT)
            cols_work[rest, :] = cols_work[rest, :] - dot3(lower, cols, NN)
    for copy in copies[12 + 2 * KCB :]:
        copy.wait()
    delta = dot3((rows_high[...], rows_low[...]), (cols_high[...], cols_low[...]), NN)
    zero = jnp.zeros((BS, BS), F32)
    for i in range(2):
        out[i, 0] = own[i]
        for j in range(2):
            out[i, 1 + j] = zero
    for i in range(4):
        out[2 + i, 0] = rows_done[col, i * BS : (i + 1) * BS, :]
        for j in range(2):
            block = child[2 + i, 1 + j] - delta[i * BS : (i + 1) * BS, j * BS : (j + 1) * BS]
            out[2 + i, 1 + j] = block
            slices[pl.ds(2 * i + j, BS, stride=16), :] = block
    for i in range(2):
        for j in range(4):
            slices[pl.ds(8 + 4 * i + j, BS, stride=16), :] = parent[i, j]


def extend_add_kernel(maps, came, out, panel_rows):
    for d in range(128):
        out[d * SLOTS : d * SLOTS + 8, :] = came[d * 16 + 8 : d * 16 + 16, :]
    for front in range(4):
        col_at = []
        for v in range(16):
            target = maps[front, v]
            col_at.append((target % 8) * SLOTS + target // 8)

        def one_row(u, carry):
            target = maps[front, u]
            row_at = (target % 16) * (8 * SLOTS) + (target // 16) * 4
            source = (front * 4 + u % 4) * (8 * 16) + (u // 4) * 2
            totals = []
            for v in range(16):
                totals.append(
                    out[pl.ds(row_at + col_at[v], 1), :]
                    + came[pl.ds(source + (v % 8) * 16 + v // 8, 1), :]
                )
            for v in range(16):
                out[pl.ds(row_at + col_at[v], 1), :] = totals[v]
            return carry

        lax.fori_loop(0, 16, one_row, 0)
    lane = lax.broadcasted_iota(jnp.int32, (1, BS), 1)
    own_at = lax.axis_index(ALL)

    def block_row(i, j):
        at = (i * 8 + j) * SLOTS
        return out[at : at + 1, :]

    rows = [block_row(0, 0), block_row(1, 1)]
    diagonals = jnp.zeros((1, BS), F32)
    for q, (i, j) in enumerate(PAIRS):
        second = block_row(j, j)
        rows.append(jnp.where(lane <= own_at, block_row(i, i), second))
        value = jnp.sum(jnp.where(lane == own_at, second, 0.0), axis=1, keepdims=True)
        diagonals = jnp.where(lane == q, value, diagonals)
    rows.append(diagonals)
    rows += [block_row(i, j) for i, j in OFF]
    for q, x in enumerate(rows):
        for half in (q // SHARE, q // SHARE + 2):
            at = KPB + q % SHARE
            panel_rows[half, at : at + 1, :] = x
    for j in range(32):
        for k in range(KPB):
            at = ((j % 16) * 8 + k) * SLOTS + (j // 16) * 4
            panel_rows[j % 4, k : k + 1, :] = out[at : at + 1, :]
        for f in range(4):
            at = ((f * 4 + j // 8) * 8 + j % 8) * SLOTS
            out[at + 8 : at + SLOTS, :] = panel_rows[j % 4]


def collect_kernel(came, own, rows, panel, pivots):
    for b in range(8):
        block = came[pl.ds(b, BS, stride=SLOTS), :]
        own[b // 4, b % 4] = block
        if b % 4 == 0:
            for d in range(8):
                rows[d, b // 4] = block
    for b in range(KPB):
        panel[b] = came[pl.ds(8 + b, BS, stride=SLOTS), :]
    for b in range(SHARE):
        pivots[b] = came[pl.ds(8 + KPB + b, BS, stride=SLOTS), :]


def own_group():
    return lax.axis_index("front") * 4 + lax.axis_index("row")


def parent_pivots_kernel(
    mine, other, lower_high, lower_low, inverse_high, inverse_low, own, work, upper, inverse, elements
):
    group, col = own_group(), own_col()
    core = lax.axis_index("core")
    here = lax.broadcasted_iota(jnp.int32, (BS, BS), 0)
    lane = lax.broadcasted_iota(jnp.int32, (BS, BS), 1)

    def received(q):
        return jnp.where(core == q // SHARE, mine[q % SHARE], other[q % SHARE])

    def place(i, j, x):
        work[i * BS : (i + 1) * BS, j * BS : (j + 1) * BS] = x

    def unpack(q, i, j):
        place(i, j, received(q))

    def unpack_lower(q, i):
        x = received(q)
        place(i, i, jnp.where(here >= lane, x, 0.0) + jnp.transpose(jnp.where(here > lane, x, 0.0)))

    def unpack_upper(q, i):
        x = jnp.where(here < lane, received(2 + q), 0.0)
        at = slice(q, q + 1)
        diagonal = jnp.where(core == 4 // SHARE, mine[4 % SHARE, :, at], other[4 % SHARE, :, at])
        place(i, i, x + jnp.transpose(x) + jnp.where(here == lane, diagonal, 0.0))

    unpack(0, 0, 0)
    waiting = [functools.partial(unpack, 5 + q, i, j) for q, (i, j) in enumerate(OFF)]
    waiting.append(functools.partial(unpack, 1, 1, 1))
    for q, (i, j) in enumerate(PAIRS):
        waiting.append(functools.partial(unpack_lower, 2 + q, i))
        waiting.append(functools.partial(unpack_upper, q, j))
    factor_pivots(
        KPB, work, upper, lower_high, lower_low, inverse, inverse_high, inverse_low, elements, waiting
    )
    row = jnp.minimum(group, KPB - 1)
    at = jnp.minimum(col, KPB - 1)
    block = work[pl.ds(pl.multiple_of(row * BS, BS), BS), pl.ds(pl.multiple_of(at * BS, BS), BS)]
    own[...] = jnp.where(row >= at, block, 0.0)


def parent_panels_kernel(
    lower_high_at, lower_low_at, inverse_high_at, inverse_low_at, rows_at,
    panel_0, panel_1, panel_2, panel_3, blocks_at, own_at,
    out,
    lower_high, lower_low, inverse_high, inverse_low, blocks, own,
    work, done, done_high, done_low, sems
):
    group, col = own_group(), own_col()
    first = [(inverse_high_at, inverse_high), (inverse_low_at, inverse_low)]
    for k in range(KPB):
        here = slice(k * BS, (k + 1) * BS)
        first += [(rows_at.at[k, i], work.at[i * BS : (i + 1) * BS, here]) for i in range(2)]
        for shift, panel in enumerate((panel_0, panel_1, panel_2, panel_3)):
            j = (lax.axis_index("row") + 4 - shift) % 4
            first.append((panel.at[k], work.at[pl.ds(pl.multiple_of((2 + j) * BS, BS), BS), here]))
    for k in range(KPB - 1):
        at = (below(k, KPB), slice(k * BS, (k + 1) * BS))
        first += [(lower_high_at.at[at], lower_high.at[at]), (lower_low_at.at[at], lower_low.at[at])]
    copies = bring(first + [(blocks_at, blocks), (own_at, own)], sems)
    for copy in copies[:38]:
        copy.wait()
    for k in range(KPB):
        here = slice(k * BS, (k + 1) * BS)
        solved = dot3(split(work[:, here]), (inverse_high[k], inverse_low[k]), NT)
        done[k] = solved[0 : 2 * BS, :]
        rows = split(solved)
        done_high[:, here] = rows[0]
        done_low[:, here] = rows[1]
        if k + 1 < KPB:
            copies[38 + 2 * k].wait()
            copies[39 + 2 * k].wait()
            rest = below(k, KPB)
            lower = (lower_high[rest, here], lower_low[rest, here])
            work[:, rest] = work[:, rest] - dot3(rows, lower, NT)
    for copy in copies[36 + 2 * KPB :]:
        copy.wait()
    left = (done_high[0 : 2 * BS, :], done_low[0 : 2 * BS, :])
    right = (done_high[2 * BS :, :], done_low[2 * BS :, :])
    delta = dot3(left, right, NT)
    at = jnp.minimum(col, KPB - 1)
    for i in range(2):
        row_pivot = group + 16 * i < KPB
        for j in range(4):
            col_pivot = col + 8 * j < KPB
            updated = blocks[i, j] - delta[i * BS : (i + 1) * BS, j * BS : (j + 1) * BS]
            if i == 0:
                updated = jnp.where(row_pivot, 0.0, updated)
            if j == 0:
                column = done[at, i * BS : (i + 1) * BS, :]
                if i == 0:
                    column = jnp.where(row_pivot, own[...], column)
                updated = jnp.where(col_pivot, column, updated)
            out[i, j] = updated


def call(kernel, outs, scratch, name, vmem, flops=0):
    def run(*args, smem=0, copies=0):
        specs = [pl.BlockSpec(memory_space=pltpu.SMEM)] * smem
        specs += [pl.BlockSpec(memory_space=pl.ANY if copies else pltpu.VMEM)] * (len(args) - smem)
        own_scratch = [pltpu.VMEM(s, t) for s, t in scratch]
        if copies:
            own_scratch.append(pltpu.SemaphoreType.DMA((copies,)))
        size = sum(a.size * a.dtype.itemsize for a in args)
        return pl.pallas_call(
            kernel,
            out_shape=[jax.ShapeDtypeStruct(s, t) for s, t in outs],
            in_specs=specs,
            out_specs=[pl.BlockSpec(memory_space=pltpu.VMEM)] * len(outs),
            scratch_shapes=own_scratch,
            compiler_params=pltpu.CompilerParams(vmem_limit_bytes=vmem * MIB),
            cost_estimate=pl.CostEstimate(flops=flops, bytes_accessed=size, transcendentals=0),
            name=name,
        )(*args)

    return run


def pivots_call(kernel, pivots, own_shape, name):
    n = pivots * BS
    return call(
        kernel,
        [((n, n), BF16), ((n, n), BF16), ((pivots, BS, BS), BF16), ((pivots, BS, BS), BF16), (own_shape, F32)],
        [((n, n), F32), ((BS, BS), F32), ((BS, BS), F32), ((2, 8, 8, BS), F32)],
        name,
        60,
        flops=30_000_000_000,
    )


def swap(x):
    return lax.ppermute(x, "core", [(0, 1), (1, 0)])


def around(x, shift):
    return lax.ppermute(x, "row", [(i, (i + shift) % 4) for i in range(4)])


def shards(child_fronts, parent_front, child_maps):
    child = child_fronts.reshape(6, 3, BS, BS)
    parent = parent_front.reshape(2, 4, BS, BS)

    payload, rows_in, cols_in = call(
        prepare_kernel,
        [((16, BS + 8, BS), F32), ((8, 4, BS, BS), F32), ((2, 2, BS, BS), F32)],
        [],
        "prepare",
        60,
    )(child)
    mine = lax.all_to_all(payload, ("row", "y"), 0, 0, tiled=True)
    other = swap(mine)
    mine, other, rows_in, cols_in = lax.optimization_barrier((mine, other, rows_in, cols_in))
    rows_in = lax.all_to_all(rows_in, COL, 0, 0, tiled=True)
    cols_in = [cols_in] + [around(cols_in, shift) for shift in (1, 2, 3)]

    factors = pivots_call(child_pivots_kernel, KCB, (2, BS, BS), "child_pivots")(mine, other)
    n = KCB * BS
    child_done, slices = call(
        child_panels_kernel,
        [((6, 3, BS, BS), F32), ((BS * 16, BS), F32)],
        [
            ((n, n), BF16), ((n, n), BF16), ((KCB, BS, BS), BF16), ((KCB, BS, BS), BF16),
            ((4, 2, 2, BS, BS), F32), ((6, 3, BS, BS), F32), ((2, BS, BS), F32), ((2, 4, BS, BS), F32),
            ((n, 256), F32), ((512, n), F32), ((KCB, 512, BS), F32),
            ((512, n), BF16), ((512, n), BF16), ((n, 256), BF16), ((n, 256), BF16),
        ],
        "child_panels",
        60,
        flops=3_000_000_000,
    )(*factors[:4], rows_in.reshape(KCB, 512, BS), *cols_in, child, factors[4], parent, copies=31)

    came = lax.all_to_all(slices.reshape(128, 16, BS), ALL, 0, 0, tiled=True)
    (sent,) = call(
        extend_add_kernel,
        [((128 * SLOTS, BS), F32)],
        [((4, KPB + SHARE, BS), F32)],
        "extend_add",
        16,
    )(child_maps, came.reshape(128 * 16, BS), smem=1)
    came = lax.all_to_all(sent.reshape(128, SLOTS, BS), ALL, 0, 0, tiled=True).reshape(128 * SLOTS, BS)
    blocks, rows_in, panel, mine = call(
        collect_kernel,
        [((2, 4, BS, BS), F32), ((8, 2, BS, BS), F32), ((KPB, BS, BS), F32), ((SHARE, BS, BS), F32)],
        [],
        "collect",
        16,
    )(came)
    other = swap(mine)
    rows_in = lax.all_to_all(rows_in, COL, 0, 0, tiled=True)
    panels = [panel] + [around(panel, shift) for shift in (1, 2, 3)]
    factors = pivots_call(parent_pivots_kernel, KPB, (BS, BS), "parent_pivots")(mine, other)
    n = KPB * BS
    (parent_done,) = call(
        parent_panels_kernel,
        [((2, 4, BS, BS), F32)],
        [
            ((n, n), BF16), ((n, n), BF16), ((KPB, BS, BS), BF16), ((KPB, BS, BS), BF16),
            ((2, 4, BS, BS), F32), ((BS, BS), F32),
            ((n, n), F32), ((KPB, 256, BS), F32), ((n, n), BF16), ((n, n), BF16),
        ],
        "parent_panels",
        60,
        flops=3_000_000_000,
    )(*factors[:4], rows_in, *panels, blocks, factors[4], copies=50)
    return child_done.reshape(child_fronts.shape), parent_done.reshape(parent_front.shape)


def solution(mesh):
    mesh = jax.sharding.Mesh(mesh.devices.reshape(4, 4, 4, 2), ALL)
    child_spec = P("front", None, "row", None, COL, None, None)
    parent_spec = P(None, ("front", "row"), None, COL, None, None)
    return jax.shard_map(
        shards,
        mesh=mesh,
        in_specs=(child_spec, parent_spec, P()),
        out_specs=(child_spec, parent_spec),
        check_vma=False,
    )
```
